256 devices in a mesh: circ: 128 (over x_lo, z, y, core), mode: 2 (over x_hi).
Axes of the slice: x: 4 (x_hi: 2, x_lo: 2; x = x_hi * 2 + x_lo), y: 4, z: 8, core: 2. Of those that a mesh axis runs over, the one named last changes fastest.
Arguments:
- right_side: float32 [20, 3, 256, 1024], P('mode', None, 'circ'), may hold values from -5 to 5
- stiffness: float32 [4, 256, 1024], P(None, 'circ'), may hold values from -0.15 to 2, as said below
- pairing: int32 [3, 20], replicated, may hold values from 0 to 19, each once within a row
- coupling: float32 [3, 20], replicated, may hold values from -1 to 1
Outputs:
- solution_field: float32 [20, 3, 256, 1024], P('mode', None, 'circ')
- residual: float32 [20, 3, 256, 1024], P('mode', None, 'circ')
The draws below stay inside these ranges and needn't reach their ends.
Inputs may be any that keep to these rules, and one draw needn't show every extreme that they name: `pairing`: each row is a permutation of the 20 chaos modes. The mean stiffness lies in [1, 2], the three random modes in [-0.15, 0.15].
All inputs are finite; a program needn't handle non-finite values.
Results may differ from the reference program's by a relative error of at most 0.001.
Values sent between devices are 32-bit elements; how exact they have to be, the bound alone decides.
A program may use at most 64 MiB of HBM per device.

```python
import math
import jax
import jax.numpy as jnp
from jax import lax

P_SIZE = 20
KM = 4
NL = 16
NT = 64
ITERS = 2
NC = 256


def draw_stiffness(key, part):
    key_mean = jax.random.fold_in(key, 11)
    key_pert = jax.random.fold_in(key, 12)
    mean_part = jax.random.uniform(key_mean, (1, NC, NL * NT), jnp.float32, 1.0, 2.0)
    pert_part = jax.random.uniform(key_pert, (KM - 1, NC, NL * NT), jnp.float32, -0.15, 0.15)
    return jnp.concatenate([mean_part, pert_part], 0)


def draw_right_side(key, part):
    key_main = jax.random.fold_in(key, 21)
    mode_ids = jnp.arange(P_SIZE, dtype=jnp.int32)
    mode_scale = jnp.where(mode_ids < P_SIZE // 2, 1.0, 0.1).astype(jnp.float32)[:, None, None, None]
    rough = jax.random.normal(key_main, (P_SIZE, 3, NC, NL * NT), jnp.float32)
    return mode_scale * jnp.clip(rough, -5.0, 5.0)


def setup_inputs(seed: int = 0) -> dict:
    seeds = jax.random.split(jax.random.key(seed), 5)
    return {
        "right_side": draw_right_side(jax.random.fold_in(seeds[4], 71), 0),
        "stiffness": draw_stiffness(jax.random.fold_in(seeds[4], 71), 0),
        "pairing": jax.vmap(lambda own: jax.random.permutation(own, P_SIZE))(jax.random.split(seeds[2], (KM - 1))).reshape((KM - 1, P_SIZE)).astype(jnp.int32),
        "coupling": jnp.clip(jax.random.uniform(seeds[3], (KM - 1, P_SIZE), jnp.float32, -1.0, 1.0), -1.0, 1.0),
    }


LAME_RATIO = 1.0


def dir_weight(component, direction):
    return 1.0 + LAME_RATIO if component == direction else 1.0


def weight_column(direction, trailing):
    values = jnp.array([dir_weight(comp_no, direction) for comp_no in range(3)], jnp.float32)
    return values.reshape((3,) + (1,) * trailing)


def stencil(padded, coeff_pad, n_long, n_trans):
    num_modes, num_comps, span_pad, num_cells = padded.shape
    span = span_pad - 2
    center = padded[:, :, 1:-1]
    coeff_mid = coeff_pad[1:-1]
    right_face = 0.5 * (coeff_mid + coeff_pad[2:])
    left_face = 0.5 * (coeff_mid + coeff_pad[:-2])
    circ_part = right_face * (center - padded[:, :, 2:]) + left_face * (center - padded[:, :, :-2])
    field = center.reshape(num_modes, num_comps, span, n_long, n_trans)
    coeff_cube = coeff_mid.reshape(span, n_long, n_trans)
    long_face = 0.5 * (coeff_cube[:, :-1] + coeff_cube[:, 1:])
    long_flux = long_face * (field[:, :, :, 1:] - field[:, :, :, :-1])
    zero_row = jnp.zeros((num_modes, num_comps, span, 1, n_trans), jnp.float32)
    long_part = jnp.concatenate([zero_row, long_flux], 3) - jnp.concatenate([long_flux, zero_row], 3)
    edge_pad = jnp.pad(coeff_cube, ((0, 0), (0, 0), (1, 1)), mode="edge")
    trans_face = 0.5 * (edge_pad[:, :, :-1] + edge_pad[:, :, 1:])
    zero_pad = jnp.pad(field, ((0, 0), (0, 0), (0, 0), (0, 0), (1, 1)))
    trans_flux = trans_face * (zero_pad[..., 1:] - zero_pad[..., :-1])
    trans_part = trans_flux[..., :-1] - trans_flux[..., 1:]
    inner = weight_column(1, 3) * long_part + weight_column(2, 3) * trans_part
    return weight_column(0, 2) * circ_part + inner.reshape(num_modes, num_comps, span, num_cells)


def build_coupling(pairing, coupling):
    modes = pairing.shape[1]
    onehot = (pairing[:, :, None] == jnp.arange(modes, dtype=jnp.int32)[None, None, :]).astype(jnp.float32)
    halfway = coupling[:, :, None] * onehot
    return 0.5 * (halfway + jnp.swapaxes(halfway, 1, 2))


def hartley_table(size):
    indices = jnp.arange(size, dtype=jnp.int32)
    product = (indices[:, None] * indices[None, :]) % size
    angle = (2.0 * math.pi / size) * product.astype(jnp.float32)
    return jnp.cos(angle) + jnp.sin(angle)


def cosine_table(size):
    indices = jnp.arange(size, dtype=jnp.int32)
    product = ((2 * indices[:, None] + 1) * indices[None, :]) % (4 * size)
    return jnp.cos((math.pi / (2 * size)) * product.astype(jnp.float32))


def sine_table(size):
    indices = jnp.arange(size, dtype=jnp.int32) + 1
    product = (indices[:, None] * indices[None, :]) % (2 * (size + 1))
    return jnp.sin((math.pi / (size + 1)) * product.astype(jnp.float32))


def eigen_denominator(freq_circ, freq_long, freq_trans, n_circ, n_long, n_trans):
    lam_circ = 2.0 - 2.0 * jnp.cos((2.0 * math.pi / n_circ) * freq_circ.astype(jnp.float32))
    lam_long = 2.0 - 2.0 * jnp.cos((math.pi / n_long) * freq_long.astype(jnp.float32))
    lam_trans = 2.0 - 2.0 * jnp.cos((math.pi / (n_trans + 1)) * (freq_trans + 1).astype(jnp.float32))
    norm_long = jnp.where(freq_long == 0, 1.0 * n_long, 0.5 * n_long).astype(jnp.float32)
    scale = n_circ * norm_long * (0.5 * (n_trans + 1))
    rows = []
    for comp_no in range(3):
        lam = dir_weight(comp_no, 0) * lam_circ + dir_weight(comp_no, 1) * lam_long + dir_weight(comp_no, 2) * lam_trans
        rows.append(lam * scale)
    return jnp.stack(rows, 0)


def precondition(values):
    num_modes, num_comps, n_circ, num_cells = values.shape
    htab = hartley_table(n_circ)
    ctab = cosine_table(NL)
    stab = sine_table(NT)
    freq_circ = jnp.arange(n_circ, dtype=jnp.int32)[:, None, None]
    freq_long = jnp.arange(NL, dtype=jnp.int32)[None, :, None]
    freq_trans = jnp.arange(NT, dtype=jnp.int32)[None, None, :]
    denom = eigen_denominator(freq_circ, freq_long, freq_trans, n_circ, NL, NT)
    hp = lax.Precision.HIGHEST
    field = values.reshape(num_modes, num_comps, n_circ, NL, NT)
    spec = jnp.einsum("pcnlt,lm->pcnmt", field, ctab, precision=hp)
    spec = jnp.einsum("pcnmt,ts->pcnms", spec, stab, precision=hp)
    spec = jnp.einsum("pcnms,nk->pckms", spec, htab, precision=hp)
    spec = spec / denom[None]
    spec = jnp.einsum("pckms,kn->pcnms", spec, htab, precision=hp)
    spec = jnp.einsum("pcnms,lm->pcnls", spec, ctab, precision=hp)
    spec = jnp.einsum("pcnls,ts->pcnlt", spec, stab, precision=hp)
    return spec.reshape(num_modes, num_comps, n_circ, num_cells)


def apply_operator(values, stiffness, gmat):
    padded = jnp.concatenate([values[:, :, -1:], values, values[:, :, :1]], 2)
    coeff_pad = jnp.concatenate([stiffness[:, -1:], stiffness, stiffness[:, :1]], 1)
    result = stencil(padded, coeff_pad[0], NL, NT)
    for order in range(1, KM):
        term = stencil(padded, coeff_pad[order], NL, NT)
        result = result + jnp.einsum("ij,jcnq->icnq", gmat[order - 1], term, precision=lax.Precision.HIGHEST)
    return result


def reference(right_side, stiffness, pairing, coupling):
    gmat = build_coupling(pairing, coupling)
    solution_field = jnp.zeros_like(right_side)
    residual = right_side
    smoothed = precondition(residual)
    direction = smoothed
    inner_now = jnp.sum(residual * smoothed)
    for iteration in range(ITERS):
        image = apply_operator(direction, stiffness, gmat)
        alpha = inner_now / jnp.sum(direction * image)
        solution_field = solution_field + alpha * direction
        residual = residual - alpha * image
        if iteration + 1 < ITERS:
            smoothed = precondition(residual)
            inner_next = jnp.sum(residual * smoothed)
            direction = smoothed + (inner_next / inner_now) * direction
            inner_now = inner_next
    return solution_field, residual
```

```python
import functools
import math

import jax
import jax.numpy as jnp
import numpy as np
from jax import lax
from jax.experimental import pallas as pl
from jax.experimental.pallas import tpu as pltpu
from jax.sharding import PartitionSpec as P

MESH = pl.DeviceIdType.MESH
HIGHEST = lax.Precision.HIGHEST
NC, NL, NT = 256, 16, 64
ROWS = 512
FIELD = (ROWS, 128)
GAMMA = 30
Z_ORDER = (4, 3, 5, 2, 6, 1, 7, 0)

T_FWD, T_INV, T_LAMK, T_LAMT, T_LAML, T_SCALE, T_W, T_SAME, T_MODE = 0, 128, 256, 512, 576, 584, 592, 600, 728


def tables():
    n = np.arange(NC)
    angle = 2.0 * np.pi / NC * ((n[:, None] * n[None, :]) % NC)
    hart = np.cos(angle) + np.sin(angle)
    ell = np.arange(NL)
    cosine = np.cos(np.pi / (2 * NL) * (((2 * ell[:, None] + 1) * ell[None, :]) % (4 * NL)))
    tee = np.arange(NT) + 1
    sine = np.sin(np.pi / (NT + 1) * ((tee[:, None] * tee[None, :]) % (2 * (NT + 1))))
    lane = np.arange(128)
    half, q = lane // 64, lane % 32
    mode, comp, valid = (lane % 64) // 32 * 10 + q // 3, q % 3, q < 30
    weight = [np.where(comp == d, 2.0, 1.0) for d in range(3)]
    table = np.zeros((856, 128))
    for a in range(8):
        for b in range(8):
            table[T_FWD + a * 8 + b] = cosine[half * 8 + b, half * 8 + a]
            table[T_FWD + 64 + a * 8 + b] = cosine[(1 - half) * 8 + b, half * 8 + a]
            table[T_INV + a * 8 + b] = cosine[half * 8 + a, half * 8 + b]
            table[T_INV + 64 + a * 8 + b] = cosine[half * 8 + a, (1 - half) * 8 + b]
    table[T_LAMK : T_LAMK + NC] = (2 - 2 * np.cos(2 * np.pi / NC * n))[:, None] * weight[0]
    table[T_LAMT : T_LAMT + NT] = (2 - 2 * np.cos(np.pi / (NT + 1) * tee))[:, None] * weight[2]
    for a in range(8):
        m = half * 8 + a
        table[T_LAML + a] = (2 - 2 * np.cos(np.pi / NL * m)) * weight[1]
        table[T_SCALE + a] = NC * np.where(m == 0, NL, NL / 2) * (NT + 1) / 2
    for d in range(3):
        table[T_W + d] = weight[d]
    table[T_W + 3] = 1.0 / weight[0]
    table[T_W + 4] = valid
    table[T_W + 5] = mode
    same = (half[:, None] == half) & (comp[:, None] == comp) & valid[:, None] & valid
    table[T_SAME : T_SAME + 128] = 0.5 * same
    table[T_MODE : T_MODE + 128] = mode[:, None]
    spread = np.zeros((8, 512))
    for k in range(4):
        for lh in range(2):
            spread[k * 2 + lh, k * 128 : (k + 1) * 128] = half == lh
    expand = (np.arange(20)[:, None] == mode) & valid
    both = np.concatenate([hart[:, 0::2], hart[:, 1::2]], 0)
    block = np.kron(np.eye(4), sine)
    return [np.asarray(v, np.float32) for v in (hart, both, block, table, spread, expand, expand.T)]


def dot(a, b):
    return jnp.dot(a, b, precision=HIGHEST, preferred_element_type=jnp.float32)


def dot_dims(a, b, ca, cb):
    return lax.dot_general(
        a, b, (((ca,), (cb,)), ((), ())), precision=HIGHEST, preferred_element_type=jnp.float32
    )


def total(v):
    return jnp.sum(jnp.sum(v, axis=0, keepdims=True), axis=1, keepdims=True)


def kernel(
    x_ref, st_ref, pair_ref, coup_ref, h_ref, both_ref, block_ref, tab, spread_ref, expand_ref, expand_t_ref,
    ox_ref, or_ref,
    xp, b_in, a_own, a_all, fsend, frecv, rsend, rrecv, sum_out, sum_in, field, zsib, ext, coef, t0, t123, rest, bt, img,
    gg, dinv, spec, tmp, out_send, out_recv, aj, ssem, rsem,
):
    circ, mode = lax.axis_index("circ"), lax.axis_index("mode")
    me = circ * 2 + mode
    xl, z, y, core = circ // 64, lax.rem(circ // 8, 8), lax.rem(circ // 2, 4), lax.rem(circ, 2)
    chip = circ // 2
    cell = 4 * chip + 2 * mode + core
    lane = lax.broadcasted_iota(jnp.int32, (1, 128), 1)
    low = lane < 64
    gamma_lane = lane == GAMMA
    valid = tab[T_W + 4 : T_W + 5, :] > 0.5

    def everyone(act):
        z_parts = [lax.rem(z + zo, 8) * 8 for zo in Z_ORDER]
        for yo in (2, 1, 3, 0):
            y_part = lax.rem(y + yo, 4) * 2

            def step(i, carry):
                k = 7 - i
                base = lax.rem(xl + k // 4, 2) * 64 + y_part + lax.rem(core + lax.rem(k // 2, 2), 2)
                there = lax.rem(mode + lax.rem(k, 2), 2)
                for part in z_parts:
                    act(base + part, there)
                return carry

            lax.fori_loop(0, 8 if yo else 7, step, 0)
        for part in z_parts[:-1]:
            act(xl * 64 + y * 2 + core + part, mode)

    def remote(src, dst, sem, where):
        pltpu.make_async_remote_copy(
            src_ref=src, dst_ref=dst, send_sem=ssem.at[sem], recv_sem=rsem.at[sem], device_id=where, device_id_type=MESH
        ).start()

    def local(src, dst, sem):
        pltpu.make_async_copy(src, dst, rsem.at[sem]).start()

    def landed(ref, sem):
        pltpu.make_async_copy(ref, ref, rsem.at[sem]).wait()

    def sent(ref, sem):
        pltpu.make_async_copy(ref, ref, ssem.at[sem]).wait()

    def pair_rows(index):
        return pl.ds(pl.multiple_of(index * 2, 2), 2)

    barrier = pltpu.get_barrier_semaphore()
    everyone(lambda c, m: pl.semaphore_signal(barrier, 1, device_id=(c, m), device_id_type=MESH))

    for part in range(4):
        xp[part * 32 + 24 : part * 32 + 32, :] = jnp.zeros((8, 512), jnp.float32)

    def load_row(r, carry):
        for e in range(2):
            for lh in range(2):
                xp[pl.ds(lh * 64 + e * 32 + r, 1), :] = x_ref[r, e : e + 1, lh * 512 : (lh + 1) * 512]
        return carry

    lax.fori_loop(0, 30, load_row, 0)
    for k in range(4):
        for e in range(2):
            for lh in range(2):
                row = k * 2 + lh
                a_own[e, row : row + 1, :] = st_ref[k, e : e + 1, lh * 512 : (lh + 1) * 512]

    def transform_t(src, dst):
        for s in (0, 256):
            dst[s : s + 256, :] = dot(block_ref[...], src[s : s + 256, :])

    def transform_l(src, dst, base, fill=None):
        def chunk(i, carry):
            at = pl.multiple_of(i * 16, 16)
            held = [src[pl.ds(at + j * 64, 16), :] for j in range(8)]
            turned = [pltpu.roll(v, 64, 1) for v in held]
            for a in range(8):
                acc = None
                for b in range(8):
                    row = base + a * 8 + b
                    term = tab[row : row + 1, :] * held[b] + tab[row + 64 : row + 65, :] * turned[b]
                    acc = term if acc is None else acc + term
                if fill is not None:
                    acc = jnp.where(gamma_lane, fill, acc)
                dst[pl.ds(at + a * 64, 16), :] = acc
            return carry

        lax.fori_loop(0, 4, chunk, 0)

    tmp[...] = jnp.transpose(xp[...])
    transform_t(tmp, t0)
    transform_l(t0, fsend.at[0], T_FWD)

    pl.semaphore_wait(barrier, 255)

    my_rows = pair_rows(mode * 128 + circ)
    everyone(lambda c, m: remote(fsend.at[0, pair_rows(c * 2 + m)], frecv.at[0, my_rows], 0, (c, m)))
    local(fsend.at[0, pair_rows(me)], frecv.at[0, my_rows], 0)

    sibling = (chip * 2 + 1 - core, mode)
    own_slot = 1 + 2 * core
    remote(a_own, a_all.at[pl.ds(own_slot, 2)], 9, sibling)
    a_all[pl.ds(own_slot, 2)] = a_own[...]
    beside = lax.rem(chip + 63 + 2 * core, 64)
    for e in range(2):
        remote(a_own.at[core], a_all.at[5 - 5 * core], 9, (beside * 2 + e, mode))
    for e in range(2):
        itself = jnp.logical_and(core == e, mode == core)
        for lh in range(2):
            src = xp.at[pl.ds(lh * 64 + e * 32, 32)]
            dst = b_in.at[pl.ds(pl.multiple_of(lh * 64 + mode * 32, 32), 32)]

            @pl.when(itself)
            def _():
                local(src, dst, 8)

            @pl.when(jnp.logical_not(itself))
            def _():
                remote(src, dst, 8, (chip * 2 + e, core))

    row_m = me // 32
    mu_l = tab[pl.ds(T_LAML + row_m, 1), :]
    scale = tab[pl.ds(T_SCALE + row_m, 1), :]
    for r in range(2):
        mu = mu_l + tab[pl.ds(T_LAMT + 2 * lax.rem(me, 32) + r, 1), :]
        dinv[:, r * 128 : (r + 1) * 128] = 1.0 / ((tab[T_LAMK : T_LAMK + 256, :] + mu) * scale)
    pairing = pair_ref[...].astype(jnp.float32)
    coupling = coup_ref[...]
    pair_row, coup_row = dot(pairing, expand_ref[...]), dot(coupling, expand_ref[...])
    pair_col, coup_col = dot_dims(expand_t_ref[...], pairing, 1, 1), dot_dims(expand_t_ref[...], coupling, 1, 1)
    mode_row, mode_col = tab[T_W + 5 : T_W + 6, :], tab[T_MODE : T_MODE + 128, :]
    for k in range(3):
        forth = jnp.where(jnp.abs(pair_col[:, k : k + 1] - mode_row) < 0.5, coup_col[:, k : k + 1], 0.0)
        back = jnp.where(jnp.abs(pair_row[k : k + 1, :] - mode_col) < 0.5, coup_row[k : k + 1, :], 0.0)
        gg[k * 128 : (k + 1) * 128, :] = tab[T_SAME : T_SAME + 128, :] * (forth + back)

    lane2 = lax.broadcasted_iota(jnp.int32, (1, 256), 1)
    first = lax.rem(lane2 // 32, 2) == 0
    real = lax.rem(lane2, 32) < 30

    def back_to_cells(sem, carried):
        weighted = spec[...] * dinv[...]
        own = total(spec[...] * weighted)
        cells = jnp.where(lane2 == GAMMA, own, dot(h_ref[...], weighted))
        for r in range(2):
            rsend[carried, pl.ds(r, 256, stride=2), :] = cells[:, r * 128 : (r + 1) * 128]
        mine = pair_rows(me)

        def act(c, m):
            there = 4 * (c // 2) + 2 * m + lax.rem(c, 2)
            remote(rsend.at[carried, pair_rows(there)], rrecv.at[carried, mine], sem, (c, m))

        everyone(act)
        local(rsend.at[carried, pair_rows(cell)], rrecv.at[carried, mine], sem)

    landed(frecv.at[0], 0)
    parts = []
    for hh in range(2):
        both = jnp.concatenate([frecv[0, pl.ds(hh * 256 + r, 128, stride=2), :] for r in range(2)], 1)
        parts.append(dot(both_ref[...], both))
    spec[...] = jnp.where(
        first,
        parts[0][:256] + pltpu.roll(parts[0][256:], 224, 1),
        parts[1][256:] + pltpu.roll(parts[1][:256], 32, 1),
    )
    back_to_cells(1, 0)

    def turned_ends(src, dst):
        dst[64:576, :] = src
        dst[0:64, :] = pltpu.roll(src[448:512], 64, 1)
        dst[576:640, :] = pltpu.roll(src[0:64], 64, 1)

    w0, w1, w2, iw0 = [tab[T_W + d : T_W + d + 1, :] for d in range(4)]
    row64 = lax.broadcasted_iota(jnp.int32, (64, 128), 0)
    lane64 = lax.broadcasted_iota(jnp.int32, (64, 128), 1)
    landed(a_all.at[pl.ds(0, 4)], 9)
    slot = 1 + 2 * mode + core
    for which, at in enumerate((slot, slot + 1 - 2 * core, slot - 1 + 2 * core)):
        aj[which] = dot_dims(a_all[at], spread_ref[...], 0, 0)
    for k in range(4):
        turned_ends(aj[0, :, k * 128 : (k + 1) * 128], ext)

        def faces(g, carry):
            at = pl.multiple_of(g * 64, 64)
            here = pl.ds(at, 64)
            a = ext[pl.ds(at + 64, 64), :]
            up, down = ext[pl.ds(at + 128, 64), :], ext[pl.ds(at, 64), :]
            sib, oth = aj[1, here, k * 128 : (k + 1) * 128], aj[2, here, k * 128 : (k + 1) * 128]
            tp = jnp.where(row64 == 63, a, pltpu.roll(a, 63, 0))
            tm = jnp.where(row64 == 0, a, pltpu.roll(a, 1, 0))
            last = jnp.logical_and(g == 7, lane64 >= 64)
            start = jnp.logical_and(g == 0, lane64 < 64)
            coef[k * 6, here, :] = (0.5 * w0) * (a + sib)
            coef[k * 6 + 1, here, :] = (0.5 * w0) * (a + oth)
            coef[k * 6 + 2, here, :] = jnp.where(last, 0.0, (0.5 * w1) * (a + up))
            coef[k * 6 + 3, here, :] = jnp.where(start, 0.0, (0.5 * w1) * (a + down))
            coef[k * 6 + 4, here, :] = (0.5 * w2) * (a + tp)
            coef[k * 6 + 5, here, :] = (0.5 * w2) * (a + tm)
            return carry

        lax.fori_loop(0, 8, faces, 0)
    landed(b_in, 8)
    bt[...] = jnp.transpose(b_in[...])

    def smoothed(n):
        landed(rrecv.at[n], 1 + 2 * n)
        carried = jnp.sum(jnp.sum(rrecv[n], axis=0, keepdims=True) * jnp.where(gamma_lane, 1.0, 0.0), axis=1, keepdims=True)
        transform_l(rrecv.at[n], tmp, T_INV)
        for s in (0, 256):
            field[n, s : s + 256, :] = jnp.where(valid, dot(block_ref[...], tmp[s : s + 256, :]), 0.0)
        remote(field.at[n], zsib.at[n], 5 + n, sibling)
        return carried

    def operator(n):
        turned_ends(field[n], ext)

        def inner(g, carry):
            at = pl.multiple_of(g * 64, 64)
            here = pl.ds(at, 64)
            v = ext[pl.ds(at + 64, 64), :]
            lp, lm = v - ext[pl.ds(at + 128, 64), :], v - ext[pl.ds(at, 64), :]
            tp = v - jnp.where(row64 == 63, 0.0, pltpu.roll(v, 63, 0))
            tm = v - jnp.where(row64 == 0, 0.0, pltpu.roll(v, 1, 0))
            for k in range(4):
                acc = (
                    coef[k * 6 + 2, here, :] * lp
                    + coef[k * 6 + 3, here, :] * lm
                    + coef[k * 6 + 4, here, :] * tp
                    + coef[k * 6 + 5, here, :] * tm
                )
                if k:
                    t123[here, (k - 1) * 128 : k * 128] = acc
                else:
                    t0[here, :] = acc
            last = jnp.logical_and(g == 7, lane64 >= 64)
            start = jnp.logical_and(g == 0, lane64 < 64)
            lap = w1 * (jnp.where(last, 0.0, lp) + jnp.where(start, 0.0, lm)) + w2 * (tp + tm) - bt[here, :]
            rest[here, :] = -(v + iw0 * lap)
            return carry

        lax.fori_loop(0, 8, inner, 0)
        landed(zsib.at[n], 5 + n)

        def outer(g, carry):
            here = pl.ds(pl.multiple_of(g * 64, 64), 64)
            sib = zsib[n, here, :]
            one, two = field[n, here, :] - sib, sib + rest[here, :]
            for k in range(4):
                acc = coef[k * 6, here, :] * one + coef[k * 6 + 1, here, :] * two
                if k:
                    t123[here, (k - 1) * 128 : k * 128] += acc
                else:
                    t0[here, :] += acc
            return carry

        lax.fori_loop(0, 8, outer, 0)
        img[n] = t0[...] + dot(t123[...], gg[...])

    def to_home(f):
        for hh in range(2):
            itself = jnp.logical_and(core == mode, mode == hh)
            for lh in range(2):
                src = out_send.at[f, pl.ds(lh * 64 + hh * 32, 32)]
                dst = out_recv.at[f, pl.ds(pl.multiple_of(lh * 64 + core * 32, 32), 32)]

                @pl.when(itself)
                def _():
                    local(src, dst, 10 + f)

                @pl.when(jnp.logical_not(itself))
                def _():
                    remote(src, dst, 10 + f, (chip * 2 + mode, hh))

    rz0 = smoothed(0)
    operator(0)
    dad = total(field[0] * img[0])

    transform_t(img.at[0], tmp)
    transform_l(tmp, fsend.at[1], T_FWD, fill=dad)
    cell_rows = pair_rows(cell)
    everyone(lambda c, m: remote(fsend.at[1, pair_rows(c * 2 + m)], frecv.at[1, cell_rows], 2, (c, m)))
    local(fsend.at[1, pair_rows(me)], frecv.at[1, cell_rows], 2)
    out_send[0] = jnp.transpose(field[0])
    to_home(0)
    out_send[1] = jnp.transpose(img[0])
    to_home(1)

    landed(frecv.at[1], 2)
    even = frecv[1, pl.ds(0, 256, stride=2), :]
    sums = jnp.sum(even, axis=0, keepdims=True)
    dad = jnp.sum(jnp.where(gamma_lane, sums, 0.0), axis=1, keepdims=True)
    alpha0 = rz0 / dad
    image_spec = dot(h_ref[...], jnp.concatenate([even, frecv[1, pl.ds(1, 256, stride=2), :]], 1))
    spec[...] = jnp.where(real, spec[...] - alpha0 * image_spec, 0.0)
    back_to_cells(3, 1)
    bt[...] = bt[...] - alpha0 * img[0]

    rz1 = smoothed(1)
    beta = rz1 / rz0
    operator(1)
    dad = total((field[1] + beta * field[0]) * (img[1] + beta * img[0]))
    sum_out[...] = jnp.broadcast_to(dad, (8, 128))
    sum_in[pl.ds(me, 1), :] = jnp.broadcast_to(dad, (1, 128))
    everyone(lambda c, m: remote(sum_out.at[pl.ds(0, 1)], sum_in.at[pl.ds(me, 1)], 4, (c, m)))
    out_send[2] = jnp.transpose(field[1])
    to_home(2)
    out_send[3] = jnp.transpose(img[1])
    to_home(3)
    landed(sum_in.at[pl.ds(0, 255)], 4)
    alpha1 = rz1 / jnp.sum(sum_in[...], axis=0, keepdims=True)[:, :1]
    both_steps = alpha0 + alpha1 * beta
    for f in range(4):
        landed(out_recv.at[f], 10 + f)
    out_recv[0] = both_steps * out_recv[0] + alpha1 * out_recv[2]
    out_recv[1] = xp[...] - both_steps * out_recv[1] - alpha1 * out_recv[3]

    def store_row(r, carry):
        for e in range(2):
            for lh in range(2):
                row = pl.ds(lh * 64 + e * 32 + r, 1)
                ox_ref[r, e : e + 1, lh * 512 : (lh + 1) * 512] = out_recv[0, row, :]
                or_ref[r, e : e + 1, lh * 512 : (lh + 1) * 512] = out_recv[1, row, :]
        return carry

    lax.fori_loop(0, 30, store_row, 0)

    for n in range(2):
        sent(fsend.at[n, pl.ds(0, 510)], 2 * n)
        sent(rsend.at[n, pl.ds(0, 510)], 1 + 2 * n)
        sent(field.at[n], 5 + n)
    sent(sum_in.at[pl.ds(0, 255)], 4)
    sent(a_all.at[pl.ds(0, 4)], 9)

    @pl.when(core == mode)
    def _():
        sent(xp.at[pl.ds(0, 64)], 8)
        for f in range(4):
            sent(out_send.at[f, pl.ds(0, 64)], 10 + f)

    @pl.when(core != mode)
    def _():
        sent(xp, 8)
        for f in range(4):
            sent(out_send.at[f], 10 + f)


def on_device(right_side, stiffness, pairing, coupling):
    consts = [jnp.asarray(v) for v in tables()]
    shape = jax.ShapeDtypeStruct((30, 2, 1024), jnp.float32)
    vmem = pl.BlockSpec(memory_space=pltpu.VMEM)
    f32 = jnp.float32
    scratch = [
        pltpu.VMEM((128, 512), f32),
        pltpu.VMEM((128, 512), f32),
        pltpu.VMEM((2, 8, 512), f32),
        pltpu.VMEM((6, 8, 512), f32),
        pltpu.VMEM((2,) + FIELD, f32),
        pltpu.VMEM((2,) + FIELD, f32),
        pltpu.VMEM((2,) + FIELD, f32),
        pltpu.VMEM((2,) + FIELD, f32),
        pltpu.VMEM((8, 128), f32),
        pltpu.VMEM((256, 128), f32),
        pltpu.VMEM((2,) + FIELD, f32),
        pltpu.VMEM((2,) + FIELD, f32),
        pltpu.VMEM((640, 128), f32),
        pltpu.VMEM((24,) + FIELD, f32),
        pltpu.VMEM(FIELD, f32),
        pltpu.VMEM((512, 384), f32),
        pltpu.VMEM(FIELD, f32),
        pltpu.VMEM(FIELD, f32),
        pltpu.VMEM((2,) + FIELD, f32),
        pltpu.VMEM((384, 128), f32),
        pltpu.VMEM((256, 256), f32),
        pltpu.VMEM((256, 256), f32),
        pltpu.VMEM(FIELD, f32),
        pltpu.VMEM((4, 128, 512), f32),
        pltpu.VMEM((4, 128, 512), f32),
        pltpu.VMEM((3, 512, 512), f32),
        pltpu.SemaphoreType.DMA((14,)),
        pltpu.SemaphoreType.DMA((14,)),
    ]
    x, r = pl.pallas_call(
        kernel,
        out_shape=(shape, shape),
        in_specs=[vmem] * 11,
        out_specs=(vmem, vmem),
        scratch_shapes=scratch,
        compiler_params=pltpu.CompilerParams(
            collective_id=0, has_side_effects=True, vmem_limit_bytes=44 * 1024 * 1024
        ),
    )(right_side.reshape(30, 2, 1024), stiffness, pairing, coupling, *consts)
    return x.reshape(right_side.shape), r.reshape(right_side.shape)


def solution(mesh):
    placed = P("mode", None, "circ", None)
    return jax.shard_map(
        on_device,
        mesh=mesh,
        in_specs=(placed, P(None, "circ", None), P(), P()),
        out_specs=(placed, placed),
        check_vma=False,
    )
```

```python
import functools
import math

import jax
import jax.numpy as jnp
import numpy as np
from jax import lax
from jax.experimental import pallas as pl
from jax.experimental.pallas import tpu as pltpu
from jax.sharding import PartitionSpec as P

MESH = pl.DeviceIdType.MESH
HIGHEST = lax.Precision.HIGHEST
NC, NL, NT = 256, 16, 64
ROWS = 512
FIELD = (ROWS, 128)
GAMMA = 30
Z_ORDER = (4, 3, 5, 2, 6, 1, 7, 0)

T_COS, T_LAMK, T_LAMT, T_LAML, T_SCALE, T_W, T_SAME, T_MODE = 0, 64, 320, 384, 392, 400, 408, 536


def tables():
    n = np.arange(NC)
    angle = 2.0 * np.pi / NC * ((n[:, None] * n[None, :]) % NC)
    hart = np.cos(angle) + np.sin(angle)
    ell = np.arange(NL)
    cosine = np.cos(np.pi / (2 * NL) * (((2 * ell[:, None] + 1) * ell[None, :]) % (4 * NL)))
    tee = np.arange(NT) + 1
    sine = np.sin(np.pi / (NT + 1) * ((tee[:, None] * tee[None, :]) % (2 * (NT + 1))))
    lane = np.arange(128)
    half, q = lane // 64, lane % 32
    mode, comp, valid = (lane % 64) // 32 * 10 + q // 3, q % 3, q < 30
    weight = [np.where(comp == d, 2.0, 1.0) for d in range(3)]
    table = np.zeros((664, 128))
    for a in range(8):
        for b in range(8):
            table[T_COS + a * 8 + b] = cosine[b, 2 * a + half]
    table[T_LAMK : T_LAMK + NC] = (2 - 2 * np.cos(2 * np.pi / NC * n))[:, None] * weight[0]
    table[T_LAMT : T_LAMT + NT] = (2 - 2 * np.cos(np.pi / (NT + 1) * tee))[:, None] * weight[2]
    for a in range(8):
        m = 2 * a + half
        table[T_LAML + a] = (2 - 2 * np.cos(np.pi / NL * m)) * weight[1]
        table[T_SCALE + a] = NC * np.where(m == 0, NL, NL / 2) * (NT + 1) / 2
    for d in range(3):
        table[T_W + d] = weight[d]
    table[T_W + 3] = 1.0 / weight[0]
    table[T_W + 4] = valid
    table[T_W + 5] = mode
    same = (half[:, None] == half) & (comp[:, None] == comp) & valid[:, None] & valid
    table[T_SAME : T_SAME + 128] = 0.5 * same
    table[T_MODE : T_MODE + 128] = mode[:, None]
    spread = np.zeros((8, 512))
    for k in range(4):
        for lh in range(2):
            spread[k * 2 + lh, k * 128 : (k + 1) * 128] = half == lh
    expand = (np.arange(20)[:, None] == mode) & valid
    both = np.concatenate([hart[:, 0::2], hart[:, 1::2]], 1)
    block = np.kron(np.eye(4), sine)
    return [np.asarray(v, np.float32) for v in (hart, both, block, table, spread, expand, expand.T)]


def dot(a, b):
    return jnp.dot(a, b, precision=HIGHEST, preferred_element_type=jnp.float32)


def dot16(a, b):
    return jnp.dot(a, b, preferred_element_type=jnp.float32)


def dot_dims(a, b, ca, cb):
    return lax.dot_general(
        a, b, (((ca,), (cb,)), ((), ())), precision=HIGHEST, preferred_element_type=jnp.float32
    )


def total(v):
    return jnp.sum(jnp.sum(v, axis=0, keepdims=True), axis=1, keepdims=True)


def kernel(
    x_far, st_far, pair_far, coup_far, h_far, both_far, block_far, tab_far, spread_far, expand_far, expand_t_far,
    y_ref,
    x_ref, st_ref, pair_ref, coup_ref, h_ref, both_ref, block_ref, tab, spread_ref, expand_ref, expand_t_ref,
    xp, b_in, a_own, a_all, fsend, frecv, rsend, rrecv, sum_out, sum_in, field, zsib, ext, coef, t0, t123, rest, bt, img,
    t_high, t_low, gg, dinv, spec, tmp, out_send, out_recv, aj, ssem, rsem, isem,
):
    fetches = {}
    for n, (src, dst) in enumerate(
        (
            (x_far, x_ref), (st_far, st_ref), (block_far, block_ref), (tab_far, tab), (pair_far, pair_ref), (coup_far, coup_ref),
            (expand_far, expand_ref), (expand_t_far, expand_t_ref), (both_far, both_ref), (h_far, h_ref), (spread_far, spread_ref),
        )
    ):
        fetches[n] = pltpu.make_async_copy(src, dst, isem.at[n])
        fetches[n].start()

    circ, mode = lax.axis_index("circ"), lax.axis_index("mode")
    me = circ * 2 + mode
    xl, z, y, core = circ // 64, lax.rem(circ // 8, 8), lax.rem(circ // 2, 4), lax.rem(circ, 2)
    chip = circ // 2
    cell = 4 * chip + 2 * mode + core
    lane = lax.broadcasted_iota(jnp.int32, (1, 128), 1)
    low = lane < 64
    gamma_lane = lane == GAMMA
    valid = lax.rem(lane, 32) < 30

    def everyone(act):
        z_parts = [lax.rem(z + zo, 8) * 8 for zo in Z_ORDER]
        for yo in (2, 1, 3, 0):
            y_part = lax.rem(y + yo, 4) * 2

            def step(i, carry):
                k = 7 - i
                base = lax.rem(xl + k // 4, 2) * 64 + y_part + lax.rem(core + lax.rem(k // 2, 2), 2)
                there = lax.rem(mode + lax.rem(k, 2), 2)
                for part in z_parts:
                    act(base + part, there)
                return carry

            lax.fori_loop(0, 8 if yo else 7, step, 0)
        for part in z_parts[:-1]:
            act(xl * 64 + y * 2 + core + part, mode)

    def remote(src, dst, sem, where):
        pltpu.make_async_remote_copy(
            src_ref=src, dst_ref=dst, send_sem=ssem.at[sem], recv_sem=rsem.at[sem], device_id=where, device_id_type=MESH
        ).start()

    def local(src, dst, sem):
        pltpu.make_async_copy(src, dst, rsem.at[sem]).start()

    def landed(ref, sem):
        pltpu.make_async_copy(ref, ref, rsem.at[sem]).wait()

    def sent(ref, sem):
        pltpu.make_async_copy(ref, ref, ssem.at[sem]).wait()

    def pair_rows(index):
        return pl.ds(pl.multiple_of(index * 2, 2), 2)

    barrier = pltpu.get_barrier_semaphore()
    everyone(lambda c, m: pl.semaphore_signal(barrier, 1, device_id=(c, m), device_id_type=MESH))

    fetches[0].wait()
    fetches[1].wait()
    for part in range(4):
        xp[part * 32 + 24 : part * 32 + 32, :] = jnp.zeros((8, 512), jnp.float32)

    def load_row(r, carry):
        for e in range(2):
            for lh in range(2):
                xp[pl.ds(lh * 64 + e * 32 + r, 1), :] = x_ref[r, e : e + 1, lh * 512 : (lh + 1) * 512]
        return carry

    lax.fori_loop(0, 30, load_row, 0)
    for k in range(4):
        for e in range(2):
            for lh in range(2):
                row = k * 2 + lh
                a_own[e, row : row + 1, :] = st_ref[k, e : e + 1, lh * 512 : (lh + 1) * 512]

    def sines(src):
        return dot(block_ref[...], jnp.concatenate([src[0:256, :], src[256:512, :]], 1))

    def transform_t(src, dst):
        out = sines(src)
        dst[0:256, :] = out[:, :128]
        dst[256:512, :] = out[:, 128:]

    def cosines_forward(src, dst, fill=None):
        def chunk(i, carry):
            at = pl.multiple_of(i * 16, 16)
            held = [src[pl.ds(at + j * 64, 16), :] for j in range(8)]
            turned = [pltpu.roll(v, 64, 1) for v in held]
            folded = [jnp.where(low, held[j] + turned[7 - j], turned[j] - held[7 - j]) for j in range(8)]
            for a in range(8):
                acc = tab[T_COS + a * 8 : T_COS + a * 8 + 1, :] * folded[0]
                for b in range(1, 8):
                    acc = acc + tab[T_COS + a * 8 + b : T_COS + a * 8 + b + 1, :] * folded[b]
                if fill is not None:
                    acc = jnp.where(gamma_lane, fill, acc)
                dst[pl.ds(at + a * 64, 16), :] = acc
            return carry

        lax.fori_loop(0, 4, chunk, 0, unroll=True)

    def cosines_back(src, dst):
        def chunk(i, carry):
            at = pl.multiple_of(i * 16, 16)
            held = [src[pl.ds(at + j * 64, 16), :] for j in range(8)]
            folded, turned = [], []
            for b in range(8):
                acc = tab[T_COS + b : T_COS + b + 1, :] * held[0]
                for a in range(1, 8):
                    acc = acc + tab[T_COS + a * 8 + b : T_COS + a * 8 + b + 1, :] * held[a]
                folded.append(acc)
                turned.append(pltpu.roll(acc, 64, 1))
            for b in range(8):
                dst[pl.ds(at + b * 64, 16), :] = jnp.where(low, folded[b] + turned[b], turned[7 - b] - folded[7 - b])
            return carry

        lax.fori_loop(0, 4, chunk, 0, unroll=True)

    tmp[...] = jnp.transpose(xp[...])
    for n in range(2, 11):
        fetches[n].wait()
    transform_t(tmp, t0)
    cosines_forward(t0, fsend.at[0])

    pl.semaphore_wait(barrier, 255)

    my_rows = pair_rows(mode * 128 + circ)
    everyone(lambda c, m: remote(fsend.at[0, pair_rows(c * 2 + m)], frecv.at[0, my_rows], 0, (c, m)))
    local(fsend.at[0, pair_rows(me)], frecv.at[0, my_rows], 0)

    sibling = (chip * 2 + 1 - core, mode)
    own_slot = 1 + 2 * core
    remote(a_own, a_all.at[pl.ds(own_slot, 2)], 9, sibling)
    a_all[pl.ds(own_slot, 2)] = a_own[...]
    beside = lax.rem(chip + 63 + 2 * core, 64)
    for e in range(2):
        remote(a_own.at[core], a_all.at[5 - 5 * core], 9, (beside * 2 + e, mode))
    for e in range(2):
        itself = jnp.logical_and(core == e, mode == core)
        for lh in range(2):
            src = xp.at[pl.ds(lh * 64 + e * 32, 32)]
            dst = b_in.at[pl.ds(pl.multiple_of(lh * 64 + mode * 32, 32), 32)]

            @pl.when(itself)
            def _():
                local(src, dst, 8)

            @pl.when(jnp.logical_not(itself))
            def _():
                remote(src, dst, 8, (chip * 2 + e, core))

    row_m = me // 32
    mu_l = tab[pl.ds(T_LAML + row_m, 1), :]
    scale = tab[pl.ds(T_SCALE + row_m, 1), :]
    for r in range(2):
        mu = mu_l + tab[pl.ds(T_LAMT + 2 * lax.rem(me, 32) + r, 1), :]
        dinv[:, r * 128 : (r + 1) * 128] = 1.0 / ((tab[T_LAMK : T_LAMK + 256, :] + mu) * scale)
    pairing = pair_ref[...].astype(jnp.float32)
    coupling = coup_ref[...]
    pair_row, coup_row = dot(pairing, expand_ref[...]), dot(coupling, expand_ref[...])
    pair_col, coup_col = dot_dims(expand_t_ref[...], pairing, 1, 1), dot_dims(expand_t_ref[...], coupling, 1, 1)
    mode_row, mode_col = tab[T_W + 5 : T_W + 6, :], tab[T_MODE : T_MODE + 128, :]
    for k in range(3):
        forth = jnp.where(jnp.abs(pair_col[:, k : k + 1] - mode_row) < 0.5, coup_col[:, k : k + 1], 0.0)
        back = jnp.where(jnp.abs(pair_row[k : k + 1, :] - mode_col) < 0.5, coup_row[k : k + 1, :], 0.0)
        whole = tab[T_SAME : T_SAME + 128, :] * (forth + back)
        high = whole.astype(jnp.bfloat16)
        gg[k * 128 : (k + 1) * 128, :128] = high
        gg[k * 128 : (k + 1) * 128, 128:] = (whole - high.astype(jnp.float32)).astype(jnp.bfloat16)

    lane2 = lax.broadcasted_iota(jnp.int32, (1, 256), 1)
    first = lax.rem(lane2 // 32, 2) == 0
    real = lax.rem(lane2, 32) < 30

    def back_to_cells(sem, carried):
        weighted = spec[...] * dinv[...]
        own = total(spec[...] * weighted)
        cells = jnp.where(lane2 == GAMMA, own, dot(h_ref[...], weighted))
        for r in range(2):
            rsend[carried, pl.ds(r, 256, stride=2), :] = cells[:, r * 128 : (r + 1) * 128]
        mine = pair_rows(me)

        def act(c, m):
            there = 4 * (c // 2) + 2 * m + lax.rem(c, 2)
            remote(rsend.at[carried, pair_rows(there)], rrecv.at[carried, mine], sem, (c, m))

        everyone(act)
        local(rsend.at[carried, pair_rows(cell)], rrecv.at[carried, mine], sem)

    landed(frecv.at[0], 0)
    arrived = [
        jnp.concatenate([frecv[0, pl.ds(hh * 256 + r, 128, stride=2), :] for r in range(2)], 1) for hh in range(2)
    ]
    even = jnp.where(first, arrived[0], pltpu.roll(arrived[1], 32, 1))
    odd = jnp.where(first, pltpu.roll(arrived[0], 224, 1), arrived[1])
    spec[...] = dot(both_ref[...], jnp.concatenate([even, odd], 0))
    back_to_cells(1, 0)

    def turned_ends(src, dst):
        dst[64:576, :] = src
        dst[0:64, :] = pltpu.roll(src[448:512], 64, 1)
        dst[576:640, :] = pltpu.roll(src[0:64], 64, 1)

    w0, w1, w2, iw0 = [tab[T_W + d : T_W + d + 1, :] for d in range(4)]
    row64 = lax.broadcasted_iota(jnp.int32, (64, 128), 0)
    lane64 = lax.broadcasted_iota(jnp.int32, (64, 128), 1)
    landed(a_all.at[pl.ds(0, 4)], 9)
    slot = 1 + 2 * mode + core
    for which, at in enumerate((slot, slot + 1 - 2 * core, slot - 1 + 2 * core)):
        aj[which] = dot_dims(a_all[at], spread_ref[...], 0, 0)
    for k in range(4):
        turned_ends(aj[0, :, k * 128 : (k + 1) * 128], ext)

        def faces(g, carry):
            at = pl.multiple_of(g * 64, 64)
            here = pl.ds(at, 64)
            a = ext[pl.ds(at + 64, 64), :]
            up, down = ext[pl.ds(at + 128, 64), :], ext[pl.ds(at, 64), :]
            sib, oth = aj[1, here, k * 128 : (k + 1) * 128], aj[2, here, k * 128 : (k + 1) * 128]
            tp = jnp.where(row64 == 63, a, pltpu.roll(a, 63, 0))
            tm = jnp.where(row64 == 0, a, pltpu.roll(a, 1, 0))
            last = jnp.logical_and(g == 7, lane64 >= 64)
            start = jnp.logical_and(g == 0, lane64 < 64)
            coef[k * 6, here, :] = (0.5 * w0) * (a + sib)
            coef[k * 6 + 1, here, :] = (0.5 * w0) * (a + oth)
            coef[k * 6 + 2, here, :] = jnp.where(last, 0.0, (0.5 * w1) * (a + up))
            coef[k * 6 + 3, here, :] = jnp.where(start, 0.0, (0.5 * w1) * (a + down))
            coef[k * 6 + 4, here, :] = (0.5 * w2) * (a + tp)
            coef[k * 6 + 5, here, :] = (0.5 * w2) * (a + tm)
            return carry

        lax.fori_loop(0, 8, faces, 0)
    landed(b_in, 8)
    bt[...] = jnp.transpose(b_in[...])

    def smoothed(n):
        landed(rrecv.at[n], 1 + 2 * n)
        carried = jnp.sum(jnp.sum(rrecv[n], axis=0, keepdims=True) * jnp.where(gamma_lane, 1.0, 0.0), axis=1, keepdims=True)
        cosines_back(rrecv.at[n], tmp)
        out = sines(tmp)
        for s in range(2):
            field[n, s * 256 : (s + 1) * 256, :] = jnp.where(valid, out[:, s * 128 : (s + 1) * 128], 0.0)
        remote(field.at[n], zsib.at[n], 5 + n, sibling)
        return carried

    def operator(n):
        turned_ends(field[n], ext)

        def inner(g, carry):
            at = pl.multiple_of(g * 64, 64)
            here = pl.ds(at, 64)
            v = ext[pl.ds(at + 64, 64), :]
            lp, lm = v - ext[pl.ds(at + 128, 64), :], v - ext[pl.ds(at, 64), :]
            tp = v - jnp.where(row64 == 63, 0.0, pltpu.roll(v, 63, 0))
            tm = v - jnp.where(row64 == 0, 0.0, pltpu.roll(v, 1, 0))
            for k in range(4):
                acc = (
                    coef[k * 6 + 2, here, :] * lp
                    + coef[k * 6 + 3, here, :] * lm
                    + coef[k * 6 + 4, here, :] * tp
                    + coef[k * 6 + 5, here, :] * tm
                )
                if k:
                    t123[here, (k - 1) * 128 : k * 128] = acc
                else:
                    t0[here, :] = acc
            last = jnp.logical_and(g == 7, lane64 >= 64)
            start = jnp.logical_and(g == 0, lane64 < 64)
            lap = w1 * (jnp.where(last, 0.0, lp) + jnp.where(start, 0.0, lm)) + w2 * (tp + tm) - bt[here, :]
            rest[here, :] = -(v + iw0 * lap)
            return carry

        lax.fori_loop(0, 8, inner, 0, unroll=True)
        landed(zsib.at[n], 5 + n)

        def outer(g, carry):
            here = pl.ds(pl.multiple_of(g * 64, 64), 64)
            sib = zsib[n, here, :]
            one, two = field[n, here, :] - sib, sib + rest[here, :]
            t0[here, :] += coef[0, here, :] * one + coef[1, here, :] * two
            for k in range(1, 4):
                at = slice((k - 1) * 128, k * 128)
                acc = t123[here, at] + coef[k * 6, here, :] * one + coef[k * 6 + 1, here, :] * two
                high = acc.astype(jnp.bfloat16)
                t_high[here, at] = high
                t_low[here, at] = (acc - high.astype(jnp.float32)).astype(jnp.bfloat16)
            return carry

        lax.fori_loop(0, 8, outer, 0, unroll=True)
        large = dot16(t_high[...], gg[...])
        img[n] = t0[...] + (large[:, :128] + (large[:, 128:] + dot16(t_low[...], gg[:, :128])))

    def to_home(f):
        for hh in range(2):
            itself = jnp.logical_and(core == mode, mode == hh)
            for lh in range(2):
                src = out_send.at[f, pl.ds(lh * 64 + hh * 32, 32)]
                dst = out_recv.at[f, pl.ds(pl.multiple_of(lh * 64 + core * 32, 32), 32)]

                @pl.when(itself)
                def _():
                    local(src, dst, 10 + f)

                @pl.when(jnp.logical_not(itself))
                def _():
                    remote(src, dst, 10 + f, (chip * 2 + mode, hh))

    rz0 = smoothed(0)
    operator(0)
    dad = total(field[0] * img[0])

    transform_t(img.at[0], tmp)
    cosines_forward(tmp, fsend.at[1], fill=dad)
    cell_rows = pair_rows(cell)
    everyone(lambda c, m: remote(fsend.at[1, pair_rows(c * 2 + m)], frecv.at[1, cell_rows], 2, (c, m)))
    local(fsend.at[1, pair_rows(me)], frecv.at[1, cell_rows], 2)
    out_send[0] = jnp.transpose(field[0])
    to_home(0)
    out_send[1] = jnp.transpose(img[0])
    to_home(1)

    landed(frecv.at[1], 2)
    even = frecv[1, pl.ds(0, 256, stride=2), :]
    sums = jnp.sum(even, axis=0, keepdims=True)
    dad = jnp.sum(jnp.where(gamma_lane, sums, 0.0), axis=1, keepdims=True)
    alpha0 = rz0 / dad
    image_spec = dot(h_ref[...], jnp.concatenate([even, frecv[1, pl.ds(1, 256, stride=2), :]], 1))
    spec[...] = jnp.where(real, spec[...] - alpha0 * image_spec, 0.0)
    back_to_cells(3, 1)
    bt[...] = bt[...] - alpha0 * img[0]

    rz1 = smoothed(1)
    beta = rz1 / rz0
    operator(1)
    dad = total((field[1] + beta * field[0]) * (img[1] + beta * img[0]))
    sum_out[...] = jnp.broadcast_to(dad, (8, 128))
    sum_in[pl.ds(me, 1), :] = jnp.broadcast_to(dad, (1, 128))
    everyone(lambda c, m: remote(sum_out.at[pl.ds(0, 1)], sum_in.at[pl.ds(me, 1)], 4, (c, m)))
    out_send[2] = jnp.transpose(field[1])
    to_home(2)
    out_send[3] = jnp.transpose(img[1])
    to_home(3)
    landed(sum_in.at[pl.ds(0, 255)], 4)
    alpha1 = rz1 / jnp.sum(sum_in[...], axis=0, keepdims=True)[:, :1]
    both_steps = alpha0 + alpha1 * beta
    for f in range(4):
        landed(out_recv.at[f], 10 + f)
    y_ref[0] = both_steps * out_recv[0] + alpha1 * out_recv[2]
    y_ref[1] = xp[...] - both_steps * out_recv[1] - alpha1 * out_recv[3]

    for n in range(2):
        sent(fsend.at[n, pl.ds(0, 510)], 2 * n)
        sent(rsend.at[n, pl.ds(0, 510)], 1 + 2 * n)
        sent(field.at[n], 5 + n)
    sent(sum_in.at[pl.ds(0, 255)], 4)
    sent(a_all.at[pl.ds(0, 4)], 9)

    @pl.when(core == mode)
    def _():
        sent(xp.at[pl.ds(0, 64)], 8)
        for f in range(4):
            sent(out_send.at[f, pl.ds(0, 64)], 10 + f)

    @pl.when(core != mode)
    def _():
        sent(xp, 8)
        for f in range(4):
            sent(out_send.at[f], 10 + f)


def unpack(y_ref, *out_refs):
    for n, out_ref in enumerate(out_refs):
        for e in range(2):
            for lh in range(2):
                at = lh * 64 + e * 32
                out_ref[:, e, lh * 512 : (lh + 1) * 512] = y_ref[n, at : at + 30, :]


def on_device(right_side, stiffness, pairing, coupling):
    consts = [jnp.asarray(v) for v in tables()]
    shape = jax.ShapeDtypeStruct((30, 2, 1024), jnp.float32)
    vmem = pl.BlockSpec(memory_space=pltpu.VMEM)
    f32 = jnp.float32
    far = pl.BlockSpec(memory_space=pltpu.HBM)
    operands = (right_side.reshape(30, 2, 1024), stiffness, pairing, coupling, *consts)
    scratch = [pltpu.VMEM(v.shape, v.dtype) for v in operands] + [
        pltpu.VMEM((128, 512), f32),
        pltpu.VMEM((128, 512), f32),
        pltpu.VMEM((2, 8, 512), f32),
        pltpu.VMEM((6, 8, 512), f32),
        pltpu.VMEM((2,) + FIELD, f32),
        pltpu.VMEM((2,) + FIELD, f32),
        pltpu.VMEM((2,) + FIELD, f32),
        pltpu.VMEM((2,) + FIELD, f32),
        pltpu.VMEM((8, 128), f32),
        pltpu.VMEM((256, 128), f32),
        pltpu.VMEM((2,) + FIELD, f32),
        pltpu.VMEM((2,) + FIELD, f32),
        pltpu.VMEM((640, 128), f32),
        pltpu.VMEM((24,) + FIELD, f32),
        pltpu.VMEM(FIELD, f32),
        pltpu.VMEM((512, 384), f32),
        pltpu.VMEM(FIELD, f32),
        pltpu.VMEM(FIELD, f32),
        pltpu.VMEM((2,) + FIELD, f32),
        pltpu.VMEM((512, 384), jnp.bfloat16),
        pltpu.VMEM((512, 384), jnp.bfloat16),
        pltpu.VMEM((384, 256), jnp.bfloat16),
        pltpu.VMEM((256, 256), f32),
        pltpu.VMEM((256, 256), f32),
        pltpu.VMEM(FIELD, f32),
        pltpu.VMEM((4, 128, 512), f32),
        pltpu.VMEM((4, 128, 512), f32),
        pltpu.VMEM((3, 512, 512), f32),
        pltpu.SemaphoreType.DMA((14,)),
        pltpu.SemaphoreType.DMA((14,)),
        pltpu.SemaphoreType.DMA((11,)),
    ]
    packed = pl.pallas_call(
        kernel,
        out_shape=jax.ShapeDtypeStruct((2, 128, 512), f32),
        in_specs=[far] * 11,
        out_specs=vmem,
        scratch_shapes=scratch,
        compiler_params=pltpu.CompilerParams(
            collective_id=0, has_side_effects=True, vmem_limit_bytes=60 * 1024 * 1024
        ),
    )(*operands)
    x, r = pl.pallas_call(unpack, out_shape=(shape, shape), in_specs=[vmem], out_specs=(vmem, vmem))(packed)
    return x.reshape(right_side.shape), r.reshape(right_side.shape)


def solution(mesh):
    placed = P("mode", None, "circ", None)
    return jax.shard_map(
        on_device,
        mesh=mesh,
        in_specs=(placed, P(None, "circ", None), P(), P()),
        out_specs=(placed, placed),
        check_vma=False,
    )
```

```python
import functools
import math

import jax
import jax.numpy as jnp
import numpy as np
from jax import lax
from jax.experimental import pallas as pl
from jax.experimental.pallas import tpu as pltpu
from jax.sharding import PartitionSpec as P

MESH = pl.DeviceIdType.MESH
HIGHEST = lax.Precision.HIGHEST
NC, NL, NT = 256, 16, 64
ROWS = 512
FIELD = (ROWS, 128)
GAMMA = 30
Z_ORDER = (4, 3, 5, 2, 6, 1, 7, 0)

T_COS, T_LAMK, T_LAMT, T_LAML, T_SCALE, T_W, T_SAME, T_MODE = 0, 64, 320, 384, 392, 400, 408, 536


def tables():
    n = np.arange(NC)
    angle = 2.0 * np.pi / NC * ((n[:, None] * n[None, :]) % NC)
    hart = np.cos(angle) + np.sin(angle)
    ell = np.arange(NL)
    cosine = np.cos(np.pi / (2 * NL) * (((2 * ell[:, None] + 1) * ell[None, :]) % (4 * NL)))
    tee = np.arange(NT) + 1
    sine = np.sin(np.pi / (NT + 1) * ((tee[:, None] * tee[None, :]) % (2 * (NT + 1))))
    lane = np.arange(128)
    half, q = lane // 64, lane % 32
    mode, comp, valid = (lane % 64) // 32 * 10 + q // 3, q % 3, q < 30
    weight = [np.where(comp == d, 2.0, 1.0) for d in range(3)]
    table = np.zeros((664, 128))
    for a in range(8):
        for b in range(8):
            table[T_COS + a * 8 + b] = cosine[b, 2 * a + half]
    table[T_LAMK : T_LAMK + NC] = (2 - 2 * np.cos(2 * np.pi / NC * n))[:, None] * weight[0]
    table[T_LAMT : T_LAMT + NT] = (2 - 2 * np.cos(np.pi / (NT + 1) * tee))[:, None] * weight[2]
    for a in range(8):
        m = 2 * a + half
        table[T_LAML + a] = (2 - 2 * np.cos(np.pi / NL * m)) * weight[1]
        table[T_SCALE + a] = NC * np.where(m == 0, NL, NL / 2) * (NT + 1) / 2
    for d in range(3):
        table[T_W + d] = weight[d]
    table[T_W + 3] = 1.0 / weight[0]
    table[T_W + 4] = valid
    table[T_W + 5] = mode
    same = (half[:, None] == half) & (comp[:, None] == comp) & valid[:, None] & valid
    table[T_SAME : T_SAME + 128] = 0.5 * same
    table[T_MODE : T_MODE + 128] = mode[:, None]
    spread = np.zeros((8, 512))
    for k in range(4):
        for lh in range(2):
            spread[k * 2 + lh, k * 128 : (k + 1) * 128] = half == lh
    expand = (np.arange(20)[:, None] == mode) & valid
    both = np.concatenate([hart[:, 0::2], hart[:, 1::2]], 1)
    block = np.kron(np.eye(4), sine)
    return [np.asarray(v, np.float32) for v in (hart, both, block, table, spread, expand, expand.T)]


def dot(a, b):
    return jnp.dot(a, b, precision=HIGHEST, preferred_element_type=jnp.float32)


def dot16(a, b):
    return jnp.dot(a, b, preferred_element_type=jnp.float32)


def dot_dims(a, b, ca, cb):
    return lax.dot_general(
        a, b, (((ca,), (cb,)), ((), ())), precision=HIGHEST, preferred_element_type=jnp.float32
    )


def total(v):
    return jnp.sum(jnp.sum(v, axis=0, keepdims=True), axis=1, keepdims=True)


def kernel(
    x_far, st_far, pair_far, coup_far, h_far, both_far, block_far, tab_far, spread_far, expand_far, expand_t_far,
    y_ref,
    x_ref, st_ref, pair_ref, coup_ref, h_ref, both_ref, block_ref, tab, spread_ref, expand_ref, expand_t_ref,
    xp, b_in, a_own, a_all, fsend, frecv, rsend, rrecv, sum_out, sum_in, field, zsib, ext, coef, t0, t123, rest, bt, img,
    t_high, t_low, gg, dinv, spec, tmp, out_send, out_recv, aj, ssem, rsem, isem,
):
    fetches = {}
    for n, (src, dst) in enumerate(
        (
            (x_far, x_ref), (st_far, st_ref), (block_far, block_ref), (tab_far, tab), (pair_far, pair_ref), (coup_far, coup_ref),
            (expand_far, expand_ref), (expand_t_far, expand_t_ref), (both_far, both_ref), (h_far, h_ref), (spread_far, spread_ref),
        )
    ):
        fetches[n] = pltpu.make_async_copy(src, dst, isem.at[n])
        fetches[n].start()

    circ, mode = lax.axis_index("circ"), lax.axis_index("mode")
    me = circ * 2 + mode
    xl, z, y, core = circ // 64, lax.rem(circ // 8, 8), lax.rem(circ // 2, 4), lax.rem(circ, 2)
    chip = circ // 2
    cell = 4 * chip + 2 * mode + core
    lane = lax.broadcasted_iota(jnp.int32, (1, 128), 1)
    low = lane < 64
    gamma_lane = lane == GAMMA
    valid = lax.rem(lane, 32) < 30

    z_parts = [lax.rem(z + zo, 8) * 8 for zo in Z_ORDER]

    def everyone(act):
        def along(base, side, there, parts):
            its_me, its_cell = base * 2 + there, base * 2 - side + there * 2
            for part in parts:
                act(base + part, there, its_me + 2 * part, its_cell + 2 * part)

        for flip in ((0, 1, 1), (0, 1, 0), (1, 1, 1), (1, 1, 0), (1, 0, 1), (1, 0, 0), (0, 0, 1), (0, 0, 0)):
            far_x, there, side = [1 - v if f else v for f, v in zip(flip, (xl, mode, core))]
            line = far_x * 64 + side

            def step(i, carry):
                along(line + lax.rem(y + 1 + i, 4) * 2, side, there, z_parts)
                return carry

            lax.fori_loop(0, 4 if any(flip) else 3, step, 0)
        along(xl * 64 + y * 2 + core, core, mode, z_parts[:-1])

    def remote(src, dst, sem, where):
        pltpu.make_async_remote_copy(
            src_ref=src, dst_ref=dst, send_sem=ssem.at[sem], recv_sem=rsem.at[sem], device_id=where, device_id_type=MESH
        ).start()

    def local(src, dst, sem):
        pltpu.make_async_copy(src, dst, rsem.at[sem]).start()

    def landed(ref, sem):
        pltpu.make_async_copy(ref, ref, rsem.at[sem]).wait()

    def sent(ref, sem):
        pltpu.make_async_copy(ref, ref, ssem.at[sem]).wait()

    def pair_rows(index):
        return pl.ds(pl.multiple_of(index * 2, 2), 2)

    barrier = pltpu.get_barrier_semaphore()
    everyone(lambda c, m, d, n: pl.semaphore_signal(barrier, 1, device_id=(c, m), device_id_type=MESH))

    fetches[0].wait()
    fetches[1].wait()
    for part in range(4):
        xp[part * 32 + 24 : part * 32 + 32, :] = jnp.zeros((8, 512), jnp.float32)

    for e in range(2):
        for lh in range(2):
            at = lh * 64 + e * 32
            xp[at : at + 30, :] = x_ref[:, e, lh * 512 : (lh + 1) * 512]
    for k in range(4):
        for e in range(2):
            for lh in range(2):
                row = k * 2 + lh
                a_own[e, row : row + 1, :] = st_ref[k, e : e + 1, lh * 512 : (lh + 1) * 512]

    def sines(src):
        return dot(block_ref[...], jnp.concatenate([src[0:256, :], src[256:512, :]], 1))

    def transform_t(src, dst):
        out = sines(src)
        dst[0:256, :] = out[:, :128]
        dst[256:512, :] = out[:, 128:]

    def cosines_forward(src, dst, fill=None):
        def chunk(i, carry):
            at = pl.multiple_of(i * 16, 16)
            held = [src[pl.ds(at + j * 64, 16), :] for j in range(8)]
            turned = [pltpu.roll(v, 64, 1) for v in held]
            folded = [jnp.where(low, held[j] + turned[7 - j], turned[j] - held[7 - j]) for j in range(8)]
            for a in range(8):
                acc = tab[T_COS + a * 8 : T_COS + a * 8 + 1, :] * folded[0]
                for b in range(1, 8):
                    acc = acc + tab[T_COS + a * 8 + b : T_COS + a * 8 + b + 1, :] * folded[b]
                if fill is not None:
                    acc = jnp.where(gamma_lane, fill, acc)
                dst[pl.ds(at + a * 64, 16), :] = acc
            return carry

        lax.fori_loop(0, 4, chunk, 0, unroll=True)

    def cosines_back(src, dst):
        def chunk(i, carry):
            at = pl.multiple_of(i * 16, 16)
            held = [src[pl.ds(at + j * 64, 16), :] for j in range(8)]
            folded, turned = [], []
            for b in range(8):
                acc = tab[T_COS + b : T_COS + b + 1, :] * held[0]
                for a in range(1, 8):
                    acc = acc + tab[T_COS + a * 8 + b : T_COS + a * 8 + b + 1, :] * held[a]
                folded.append(acc)
                turned.append(pltpu.roll(acc, 64, 1))
            for b in range(8):
                dst[pl.ds(at + b * 64, 16), :] = jnp.where(low, folded[b] + turned[b], turned[7 - b] - folded[7 - b])
            return carry

        lax.fori_loop(0, 4, chunk, 0, unroll=True)

    tmp[...] = jnp.transpose(xp[...])
    for n in range(2, 11):
        fetches[n].wait()
    transform_t(tmp, t0)
    cosines_forward(t0, fsend.at[0])

    pl.semaphore_wait(barrier, 255)

    my_rows = pair_rows(mode * 128 + circ)
    everyone(lambda c, m, d, n: remote(fsend.at[0, pair_rows(d)], frecv.at[0, my_rows], 0, (c, m)))
    local(fsend.at[0, pair_rows(me)], frecv.at[0, my_rows], 0)

    sibling = (chip * 2 + 1 - core, mode)
    own_slot = 1 + 2 * core
    remote(a_own, a_all.at[pl.ds(own_slot, 2)], 9, sibling)
    a_all[pl.ds(own_slot, 2)] = a_own[...]
    beside = lax.rem(chip + 63 + 2 * core, 64)
    for e in range(2):
        remote(a_own.at[core], a_all.at[5 - 5 * core], 9, (beside * 2 + e, mode))
    for e in range(2):
        itself = jnp.logical_and(core == e, mode == core)
        for lh in range(2):
            src = xp.at[pl.ds(lh * 64 + e * 32, 32)]
            dst = b_in.at[pl.ds(pl.multiple_of(lh * 64 + mode * 32, 32), 32)]

            @pl.when(itself)
            def _():
                local(src, dst, 8)

            @pl.when(jnp.logical_not(itself))
            def _():
                remote(src, dst, 8, (chip * 2 + e, core))

    row_m = me // 32
    mu_l = tab[pl.ds(T_LAML + row_m, 1), :]
    scale = tab[pl.ds(T_SCALE + row_m, 1), :]
    for r in range(2):
        mu = mu_l + tab[pl.ds(T_LAMT + 2 * lax.rem(me, 32) + r, 1), :]
        dinv[:, r * 128 : (r + 1) * 128] = 1.0 / ((tab[T_LAMK : T_LAMK + 256, :] + mu) * scale)
    pairing = pair_ref[...].astype(jnp.float32)
    coupling = coup_ref[...]
    pair_row, coup_row = dot(pairing, expand_ref[...]), dot(coupling, expand_ref[...])
    pair_col, coup_col = dot_dims(expand_t_ref[...], pairing, 1, 1), dot_dims(expand_t_ref[...], coupling, 1, 1)
    mode_row, mode_col = tab[T_W + 5 : T_W + 6, :], tab[T_MODE : T_MODE + 128, :]
    for k in range(3):
        forth = jnp.where(jnp.abs(pair_col[:, k : k + 1] - mode_row) < 0.5, coup_col[:, k : k + 1], 0.0)
        back = jnp.where(jnp.abs(pair_row[k : k + 1, :] - mode_col) < 0.5, coup_row[k : k + 1, :], 0.0)
        whole = tab[T_SAME : T_SAME + 128, :] * (forth + back)
        high = whole.astype(jnp.bfloat16)
        gg[k * 128 : (k + 1) * 128, :128] = high
        gg[k * 128 : (k + 1) * 128, 128:] = (whole - high.astype(jnp.float32)).astype(jnp.bfloat16)

    lane2 = lax.broadcasted_iota(jnp.int32, (1, 256), 1)
    first = lax.rem(lane2 // 32, 2) == 0
    real = lax.rem(lane2, 32) < 30

    def back_to_cells(sem, carried):
        weighted = spec[...] * dinv[...]
        own = total(spec[...] * weighted)
        cells = jnp.where(lane2 == GAMMA, own, dot(h_ref[...], weighted))
        for r in range(2):
            rsend[carried, pl.ds(r, 256, stride=2), :] = cells[:, r * 128 : (r + 1) * 128]
        mine = pair_rows(me)

        everyone(
            lambda c, m, d, n: remote(rsend.at[carried, pair_rows(n)], rrecv.at[carried, mine], sem, (c, m))
        )
        local(rsend.at[carried, pair_rows(cell)], rrecv.at[carried, mine], sem)

    landed(frecv.at[0], 0)
    arrived = [
        jnp.concatenate([frecv[0, pl.ds(hh * 256 + r, 128, stride=2), :] for r in range(2)], 1) for hh in range(2)
    ]
    even = jnp.where(first, arrived[0], pltpu.roll(arrived[1], 32, 1))
    odd = jnp.where(first, pltpu.roll(arrived[0], 224, 1), arrived[1])
    spec[...] = dot(both_ref[...], jnp.concatenate([even, odd], 0))
    back_to_cells(1, 0)

    def turned_ends(src, dst):
        dst[64:576, :] = src
        dst[0:64, :] = pltpu.roll(src[448:512], 64, 1)
        dst[576:640, :] = pltpu.roll(src[0:64], 64, 1)

    w0, w1, w2, iw0 = [tab[T_W + d : T_W + d + 1, :] for d in range(4)]
    row64 = lax.broadcasted_iota(jnp.int32, (64, 128), 0)
    lane64 = lax.broadcasted_iota(jnp.int32, (64, 128), 1)
    landed(a_all.at[pl.ds(0, 4)], 9)
    slot = 1 + 2 * mode + core
    for which, at in enumerate((slot, slot + 1 - 2 * core, slot - 1 + 2 * core)):
        aj[which] = dot_dims(a_all[at], spread_ref[...], 0, 0)
    for k in range(4):
        turned_ends(aj[0, :, k * 128 : (k + 1) * 128], ext)

        def faces(g, carry):
            at = pl.multiple_of(g * 64, 64)
            here = pl.ds(at, 64)
            a = ext[pl.ds(at + 64, 64), :]
            up, down = ext[pl.ds(at + 128, 64), :], ext[pl.ds(at, 64), :]
            sib, oth = aj[1, here, k * 128 : (k + 1) * 128], aj[2, here, k * 128 : (k + 1) * 128]
            tp = jnp.where(row64 == 63, a, pltpu.roll(a, 63, 0))
            tm = jnp.where(row64 == 0, a, pltpu.roll(a, 1, 0))
            last = jnp.logical_and(g == 7, lane64 >= 64)
            start = jnp.logical_and(g == 0, lane64 < 64)
            coef[k * 6, here, :] = (0.5 * w0) * (a + sib)
            coef[k * 6 + 1, here, :] = (0.5 * w0) * (a + oth)
            coef[k * 6 + 2, here, :] = jnp.where(last, 0.0, (0.5 * w1) * (a + up))
            coef[k * 6 + 3, here, :] = jnp.where(start, 0.0, (0.5 * w1) * (a + down))
            coef[k * 6 + 4, here, :] = (0.5 * w2) * (a + tp)
            coef[k * 6 + 5, here, :] = (0.5 * w2) * (a + tm)
            return carry

        lax.fori_loop(0, 8, faces, 0)
    landed(b_in, 8)
    bt[...] = jnp.transpose(b_in[...])

    def smoothed(n):
        landed(rrecv.at[n], 1 + 2 * n)
        carried = jnp.sum(jnp.sum(rrecv[n], axis=0, keepdims=True) * jnp.where(gamma_lane, 1.0, 0.0), axis=1, keepdims=True)
        cosines_back(rrecv.at[n], tmp)
        out = sines(tmp)
        for s in range(2):
            part = pl.ds(s * 256, 256)
            field[n, part, :] = jnp.where(valid, out[:, s * 128 : (s + 1) * 128], 0.0)
            remote(field.at[n, part], zsib.at[n, part], (5 if s == 0 else 14) + n, sibling)
        return carried

    def operator(n):
        turned_ends(field[n], ext)

        def inner(g, carry):
            at = pl.multiple_of(g * 64, 64)
            here = pl.ds(at, 64)
            v = ext[pl.ds(at + 64, 64), :]
            lp, lm = v - ext[pl.ds(at + 128, 64), :], v - ext[pl.ds(at, 64), :]
            tp = v - jnp.where(row64 == 63, 0.0, pltpu.roll(v, 63, 0))
            tm = v - jnp.where(row64 == 0, 0.0, pltpu.roll(v, 1, 0))
            for k in range(4):
                acc = (
                    coef[k * 6 + 2, here, :] * lp
                    + coef[k * 6 + 3, here, :] * lm
                    + coef[k * 6 + 4, here, :] * tp
                    + coef[k * 6 + 5, here, :] * tm
                )
                if k:
                    t123[here, (k - 1) * 128 : k * 128] = acc
                else:
                    t0[here, :] = acc
            last = jnp.logical_and(g == 7, lane64 >= 64)
            start = jnp.logical_and(g == 0, lane64 < 64)
            lap = w1 * (jnp.where(last, 0.0, lp) + jnp.where(start, 0.0, lm)) + w2 * (tp + tm) - bt[here, :]
            rest[here, :] = -(v + iw0 * lap)
            return carry

        lax.fori_loop(0, 8, inner, 0, unroll=True)

        def outer(g, carry):
            here = pl.ds(pl.multiple_of(g * 64, 64), 64)
            sib = zsib[n, here, :]
            one, two = field[n, here, :] - sib, sib + rest[here, :]
            t0[here, :] += coef[0, here, :] * one + coef[1, here, :] * two
            for k in range(1, 4):
                at = slice((k - 1) * 128, k * 128)
                acc = t123[here, at] + coef[k * 6, here, :] * one + coef[k * 6 + 1, here, :] * two
                high = acc.astype(jnp.bfloat16)
                t_high[here, at] = high
                t_low[here, at] = (acc - high.astype(jnp.float32)).astype(jnp.bfloat16)
            return carry

        for s in range(2):
            landed(zsib.at[n, pl.ds(s * 256, 256)], (5 if s == 0 else 14) + n)
            lax.fori_loop(4 * s, 4 * s + 4, outer, 0, unroll=True)
        large = dot16(t_high[...], gg[...])
        img[n] = t0[...] + (large[:, :128] + (large[:, 128:] + dot16(t_low[...], gg[:, :128])))

    def to_home(f):
        for hh in range(2):
            itself = jnp.logical_and(core == mode, mode == hh)
            for lh in range(2):
                src = out_send.at[f, pl.ds(lh * 64 + hh * 32, 32)]
                dst = out_recv.at[f, pl.ds(pl.multiple_of(lh * 64 + core * 32, 32), 32)]

                @pl.when(itself)
                def _():
                    local(src, dst, 10 + f)

                @pl.when(jnp.logical_not(itself))
                def _():
                    remote(src, dst, 10 + f, (chip * 2 + mode, hh))

    rz0 = smoothed(0)
    operator(0)
    dad = total(field[0] * img[0])

    transform_t(img.at[0], tmp)
    cosines_forward(tmp, fsend.at[1], fill=dad)
    cell_rows = pair_rows(cell)
    everyone(lambda c, m, d, n: remote(fsend.at[1, pair_rows(d)], frecv.at[1, cell_rows], 2, (c, m)))
    local(fsend.at[1, pair_rows(me)], frecv.at[1, cell_rows], 2)
    out_send[0] = jnp.transpose(field[0])
    to_home(0)
    out_send[1] = jnp.transpose(img[0])
    to_home(1)

    landed(frecv.at[1], 2)
    even = frecv[1, pl.ds(0, 256, stride=2), :]
    sums = jnp.sum(even, axis=0, keepdims=True)
    dad = jnp.sum(jnp.where(gamma_lane, sums, 0.0), axis=1, keepdims=True)
    alpha0 = rz0 / dad
    image_spec = dot(h_ref[...], jnp.concatenate([even, frecv[1, pl.ds(1, 256, stride=2), :]], 1))
    spec[...] = jnp.where(real, spec[...] - alpha0 * image_spec, 0.0)
    back_to_cells(3, 1)
    bt[...] = bt[...] - alpha0 * img[0]

    rz1 = smoothed(1)
    beta = rz1 / rz0
    operator(1)
    dad = total((field[1] + beta * field[0]) * (img[1] + beta * img[0]))
    sum_out[...] = jnp.broadcast_to(dad, (8, 128))
    sum_in[pl.ds(me, 1), :] = jnp.broadcast_to(dad, (1, 128))
    everyone(lambda c, m, d, n: remote(sum_out.at[pl.ds(0, 1)], sum_in.at[pl.ds(me, 1)], 4, (c, m)))
    out_send[2] = jnp.transpose(field[1])
    to_home(2)
    out_send[3] = jnp.transpose(img[1])
    to_home(3)
    landed(sum_in.at[pl.ds(0, 255)], 4)
    alpha1 = rz1 / jnp.sum(sum_in[...], axis=0, keepdims=True)[:, :1]
    both_steps = alpha0 + alpha1 * beta
    for f in range(4):
        landed(out_recv.at[f], 10 + f)
    y_ref[0] = both_steps * out_recv[0] + alpha1 * out_recv[2]
    y_ref[1] = xp[...] - both_steps * out_recv[1] - alpha1 * out_recv[3]

    for n in range(2):
        sent(fsend.at[n, pl.ds(0, 510)], 2 * n)
        sent(rsend.at[n, pl.ds(0, 510)], 1 + 2 * n)
        sent(field.at[n, pl.ds(0, 256)], 5 + n)
        sent(field.at[n, pl.ds(256, 256)], 14 + n)
    sent(sum_in.at[pl.ds(0, 255)], 4)
    sent(a_all.at[pl.ds(0, 4)], 9)

    @pl.when(core == mode)
    def _():
        sent(xp.at[pl.ds(0, 64)], 8)
        for f in range(4):
            sent(out_send.at[f, pl.ds(0, 64)], 10 + f)

    @pl.when(core != mode)
    def _():
        sent(xp, 8)
        for f in range(4):
            sent(out_send.at[f], 10 + f)


def unpack(y_ref, *out_refs):
    for n, out_ref in enumerate(out_refs):
        for e in range(2):
            for lh in range(2):
                at = lh * 64 + e * 32
                out_ref[:, e, lh * 512 : (lh + 1) * 512] = y_ref[n, at : at + 30, :]


def on_device(right_side, stiffness, pairing, coupling):
    consts = [jnp.asarray(v) for v in tables()]
    shape = jax.ShapeDtypeStruct((30, 2, 1024), jnp.float32)
    vmem = pl.BlockSpec(memory_space=pltpu.VMEM)
    f32 = jnp.float32
    far = pl.BlockSpec(memory_space=pltpu.HBM)
    operands = (right_side.reshape(30, 2, 1024), stiffness, pairing, coupling, *consts)
    scratch = [pltpu.VMEM(v.shape, v.dtype) for v in operands] + [
        pltpu.VMEM((128, 512), f32),
        pltpu.VMEM((128, 512), f32),
        pltpu.VMEM((2, 8, 512), f32),
        pltpu.VMEM((6, 8, 512), f32),
        pltpu.VMEM((2,) + FIELD, f32),
        pltpu.VMEM((2,) + FIELD, f32),
        pltpu.VMEM((2,) + FIELD, f32),
        pltpu.VMEM((2,) + FIELD, f32),
        pltpu.VMEM((8, 128), f32),
        pltpu.VMEM((256, 128), f32),
        pltpu.VMEM((2,) + FIELD, f32),
        pltpu.VMEM((2,) + FIELD, f32),
        pltpu.VMEM((640, 128), f32),
        pltpu.VMEM((24,) + FIELD, f32),
        pltpu.VMEM(FIELD, f32),
        pltpu.VMEM((512, 384), f32),
        pltpu.VMEM(FIELD, f32),
        pltpu.VMEM(FIELD, f32),
        pltpu.VMEM((2,) + FIELD, f32),
        pltpu.VMEM((512, 384), jnp.bfloat16),
        pltpu.VMEM((512, 384), jnp.bfloat16),
        pltpu.VMEM((384, 256), jnp.bfloat16),
        pltpu.VMEM((256, 256), f32),
        pltpu.VMEM((256, 256), f32),
        pltpu.VMEM(FIELD, f32),
        pltpu.VMEM((4, 128, 512), f32),
        pltpu.VMEM((4, 128, 512), f32),
        pltpu.VMEM((3, 512, 512), f32),
        pltpu.SemaphoreType.DMA((16,)),
        pltpu.SemaphoreType.DMA((16,)),
        pltpu.SemaphoreType.DMA((11,)),
    ]
    packed = pl.pallas_call(
        kernel,
        out_shape=jax.ShapeDtypeStruct((2, 128, 512), f32),
        in_specs=[far] * 11,
        out_specs=vmem,
        scratch_shapes=scratch,
        compiler_params=pltpu.CompilerParams(
            collective_id=0, has_side_effects=True, vmem_limit_bytes=60 * 1024 * 1024
        ),
    )(*operands)
    x, r = pl.pallas_call(unpack, out_shape=(shape, shape), in_specs=[vmem], out_specs=(vmem, vmem))(packed)
    return x.reshape(right_side.shape), r.reshape(right_side.shape)


def solution(mesh):
    placed = P("mode", None, "circ", None)
    return jax.shard_map(
        on_device,
        mesh=mesh,
        in_specs=(placed, P(None, "circ", None), P(), P()),
        out_specs=(placed, placed),
        check_vma=False,
    )
```

```python
import functools
import math

import jax
import jax.numpy as jnp
import numpy as np
from jax import lax
from jax.experimental import pallas as pl
from jax.experimental.pallas import tpu as pltpu
from jax.sharding import PartitionSpec as P

MESH = pl.DeviceIdType.MESH
HIGHEST = lax.Precision.HIGHEST
NC, NL, NT = 256, 16, 64
ROWS = 512
FIELD = (ROWS, 128)
GAMMA = 30
Z_ORDER = (4, 3, 5, 2, 6, 1, 7, 0)

T_COS, T_LAMK, T_LAMT, T_LAML, T_SCALE, T_W, T_SAME, T_MODE = 0, 64, 320, 384, 392, 400, 408, 536


def tables():
    n = np.arange(NC)
    angle = 2.0 * np.pi / NC * ((n[:, None] * n[None, :]) % NC)
    hart = np.cos(angle) + np.sin(angle)
    ell = np.arange(NL)
    cosine = np.cos(np.pi / (2 * NL) * (((2 * ell[:, None] + 1) * ell[None, :]) % (4 * NL)))
    tee = np.arange(NT) + 1
    sine = np.sin(np.pi / (NT + 1) * ((tee[:, None] * tee[None, :]) % (2 * (NT + 1))))
    lane = np.arange(128)
    half, q = lane // 64, lane % 32
    mode, comp, valid = (lane % 64) // 32 * 10 + q // 3, q % 3, q < 30
    weight = [np.where(comp == d, 2.0, 1.0) for d in range(3)]
    table = np.zeros((664, 128))
    for a in range(8):
        for b in range(8):
            table[T_COS + a * 8 + b] = cosine[b, 2 * a + half]
    table[T_LAMK : T_LAMK + NC] = (2 - 2 * np.cos(2 * np.pi / NC * n))[:, None] * weight[0]
    table[T_LAMT : T_LAMT + NT] = (2 - 2 * np.cos(np.pi / (NT + 1) * tee))[:, None] * weight[2]
    for a in range(8):
        m = 2 * a + half
        table[T_LAML + a] = (2 - 2 * np.cos(np.pi / NL * m)) * weight[1]
        table[T_SCALE + a] = NC * np.where(m == 0, NL, NL / 2) * (NT + 1) / 2
    for d in range(3):
        table[T_W + d] = weight[d]
    table[T_W + 3] = 1.0 / weight[0]
    table[T_W + 4] = valid
    table[T_W + 5] = mode
    same = (half[:, None] == half) & (comp[:, None] == comp) & valid[:, None] & valid
    table[T_SAME : T_SAME + 128] = 0.5 * same
    table[T_MODE : T_MODE + 128] = mode[:, None]
    spread = np.zeros((8, 512))
    for k in range(4):
        for lh in range(2):
            spread[k * 2 + lh, k * 128 : (k + 1) * 128] = half == lh
    expand = (np.arange(20)[:, None] == mode) & valid
    both = np.concatenate([hart[:, 0::2], hart[:, 1::2]], 1)
    block = np.kron(np.eye(4), sine)
    return [np.asarray(v, np.float32) for v in (hart, both, block, table, spread, expand, expand.T)]


def dot(a, b):
    return jnp.dot(a, b, precision=HIGHEST, preferred_element_type=jnp.float32)


def dot16(a, b):
    return jnp.dot(a, b, preferred_element_type=jnp.float32)


def dot_dims(a, b, ca, cb):
    return lax.dot_general(
        a, b, (((ca,), (cb,)), ((), ())), precision=HIGHEST, preferred_element_type=jnp.float32
    )


def total(v):
    return jnp.sum(jnp.sum(v, axis=0, keepdims=True), axis=1, keepdims=True)


def kernel(
    x_far, st_far, pair_far, coup_far, h_far, both_far, block_far, tab_far, spread_far, expand_far, expand_t_far,
    y_ref,
    x_ref, st_ref, pair_ref, coup_ref, h_ref, both_ref, block_ref, tab, spread_ref, expand_ref, expand_t_ref,
    xp, b_in, a_own, a_all, fsend, frecv, rsend, rrecv, sum_out, sum_in, field, zsib, ext, coef, t0, t123, rest, bt, img,
    t_high, t_low, gg, dinv, spec, tmp, out_send, out_recv, aj, ssem, rsem, isem,
):
    fetches = {}
    for n, (src, dst) in enumerate(
        (
            (x_far, x_ref), (st_far, st_ref), (block_far, block_ref), (tab_far, tab), (pair_far, pair_ref), (coup_far, coup_ref),
            (expand_far, expand_ref), (expand_t_far, expand_t_ref), (both_far, both_ref), (h_far, h_ref), (spread_far, spread_ref),
        )
    ):
        fetches[n] = pltpu.make_async_copy(src, dst, isem.at[n])
        fetches[n].start()

    circ, mode = lax.axis_index("circ"), lax.axis_index("mode")
    me = circ * 2 + mode
    xl, z, y, core = circ // 64, lax.rem(circ // 8, 8), lax.rem(circ // 2, 4), lax.rem(circ, 2)
    chip = circ // 2
    cell = 4 * chip + 2 * mode + core
    lane = lax.broadcasted_iota(jnp.int32, (1, 128), 1)
    low = lane < 64
    gamma_lane = lane == GAMMA
    valid = lax.rem(lane, 32) < 30

    z_parts = [lax.rem(z + zo, 8) * 8 for zo in Z_ORDER]

    def everyone(act):
        def along(base, side, there, parts):
            its_me, its_cell = base * 2 + there, base * 2 - side + there * 2
            for part in parts:
                act(base + part, there, its_me + 2 * part, its_cell + 2 * part)

        for flip in ((0, 1, 1), (0, 1, 0), (1, 1, 1), (1, 1, 0), (1, 0, 1), (1, 0, 0), (0, 0, 1), (0, 0, 0)):
            far_x, there, side = [1 - v if f else v for f, v in zip(flip, (xl, mode, core))]
            line = far_x * 64 + side

            def step(i, carry):
                along(line + lax.rem(y + 1 + i, 4) * 2, side, there, z_parts)
                return carry

            lax.fori_loop(0, 4 if any(flip) else 3, step, 0)
        along(xl * 64 + y * 2 + core, core, mode, z_parts[:-1])

    def remote(src, dst, sem, where):
        pltpu.make_async_remote_copy(
            src_ref=src, dst_ref=dst, send_sem=ssem.at[sem], recv_sem=rsem.at[sem], device_id=where, device_id_type=MESH
        ).start()

    def local(src, dst, sem):
        pltpu.make_async_copy(src, dst, rsem.at[sem]).start()

    def landed(ref, sem):
        pltpu.make_async_copy(ref, ref, rsem.at[sem]).wait()

    def sent(ref, sem):
        pltpu.make_async_copy(ref, ref, ssem.at[sem]).wait()

    def pair_rows(index):
        return pl.ds(pl.multiple_of(index * 2, 2), 2)

    barrier = pltpu.get_barrier_semaphore()
    everyone(lambda c, m, d, n: pl.semaphore_signal(barrier, 1, device_id=(c, m), device_id_type=MESH))

    fetches[0].wait()
    fetches[1].wait()
    for part in range(4):
        xp[part * 32 + 24 : part * 32 + 32, :] = jnp.zeros((8, 512), jnp.float32)

    for e in range(2):
        for lh in range(2):
            at = lh * 64 + e * 32
            xp[at : at + 30, :] = x_ref[:, e, lh * 512 : (lh + 1) * 512]
    for k in range(4):
        for e in range(2):
            for lh in range(2):
                row = k * 2 + lh
                a_own[e, row : row + 1, :] = st_ref[k, e : e + 1, lh * 512 : (lh + 1) * 512]

    def sines(src):
        return dot(block_ref[...], jnp.concatenate([src[0:256, :], src[256:512, :]], 1))

    def transform_t(src, dst):
        out = sines(src)
        dst[0:256, :] = out[:, :128]
        dst[256:512, :] = out[:, 128:]

    def cosines_forward(src, dst, fill=None):
        def chunk(i, carry):
            at = pl.multiple_of(i * 16, 16)
            held = [src[pl.ds(at + j * 64, 16), :] for j in range(8)]
            turned = [pltpu.roll(v, 64, 1) for v in held]
            folded = [jnp.where(low, held[j] + turned[7 - j], turned[j] - held[7 - j]) for j in range(8)]
            for a in range(8):
                acc = tab[T_COS + a * 8 : T_COS + a * 8 + 1, :] * folded[0]
                for b in range(1, 8):
                    acc = acc + tab[T_COS + a * 8 + b : T_COS + a * 8 + b + 1, :] * folded[b]
                if fill is not None:
                    acc = jnp.where(gamma_lane, fill, acc)
                dst[pl.ds(at + a * 64, 16), :] = acc
            return carry

        lax.fori_loop(0, 4, chunk, 0, unroll=True)

    def cosines_back(src, dst):
        def chunk(i, carry):
            at = pl.multiple_of(i * 16, 16)
            held = [src[pl.ds(at + j * 64, 16), :] for j in range(8)]
            folded, turned = [], []
            for b in range(8):
                acc = tab[T_COS + b : T_COS + b + 1, :] * held[0]
                for a in range(1, 8):
                    acc = acc + tab[T_COS + a * 8 + b : T_COS + a * 8 + b + 1, :] * held[a]
                folded.append(acc)
                turned.append(pltpu.roll(acc, 64, 1))
            for b in range(8):
                dst[pl.ds(at + b * 64, 16), :] = jnp.where(low, folded[b] + turned[b], turned[7 - b] - folded[7 - b])
            return carry

        lax.fori_loop(0, 4, chunk, 0, unroll=True)

    tmp[...] = jnp.transpose(xp[...])
    for n in range(2, 11):
        fetches[n].wait()
    transform_t(tmp, t0)
    cosines_forward(t0, fsend.at[0])

    pl.semaphore_wait(barrier, 255)

    my_rows = pair_rows(mode * 128 + circ)
    everyone(lambda c, m, d, n: remote(fsend.at[0, pair_rows(d)], frecv.at[0, my_rows], 0, (c, m)))
    local(fsend.at[0, pair_rows(me)], frecv.at[0, my_rows], 0)

    sibling = (chip * 2 + 1 - core, mode)
    own_slot = 1 + 2 * core
    remote(a_own, a_all.at[pl.ds(own_slot, 2)], 9, sibling)
    a_all[pl.ds(own_slot, 2)] = a_own[...]
    beside = lax.rem(chip + 63 + 2 * core, 64)
    for e in range(2):
        remote(a_own.at[core], a_all.at[5 - 5 * core], 9, (beside * 2 + e, mode))
    for e in range(2):
        itself = jnp.logical_and(core == e, mode == core)
        for lh in range(2):
            src = xp.at[pl.ds(lh * 64 + e * 32, 32)]
            dst = b_in.at[pl.ds(pl.multiple_of(lh * 64 + mode * 32, 32), 32)]

            @pl.when(itself)
            def _():
                local(src, dst, 8)

            @pl.when(jnp.logical_not(itself))
            def _():
                remote(src, dst, 8, (chip * 2 + e, core))

    row_m = me // 32
    mu_l = tab[pl.ds(T_LAML + row_m, 1), :]
    scale = tab[pl.ds(T_SCALE + row_m, 1), :]
    for r in range(2):
        mu = mu_l + tab[pl.ds(T_LAMT + 2 * lax.rem(me, 32) + r, 1), :]
        dinv[:, r * 128 : (r + 1) * 128] = 1.0 / ((tab[T_LAMK : T_LAMK + 256, :] + mu) * scale)
    pairing = pair_ref[...].astype(jnp.float32)
    coupling = coup_ref[...]
    pair_row, coup_row = dot(pairing, expand_ref[...]), dot(coupling, expand_ref[...])
    pair_col, coup_col = dot_dims(expand_t_ref[...], pairing, 1, 1), dot_dims(expand_t_ref[...], coupling, 1, 1)
    mode_row, mode_col = tab[T_W + 5 : T_W + 6, :], tab[T_MODE : T_MODE + 128, :]
    for k in range(3):
        forth = jnp.where(jnp.abs(pair_col[:, k : k + 1] - mode_row) < 0.5, coup_col[:, k : k + 1], 0.0)
        back = jnp.where(jnp.abs(pair_row[k : k + 1, :] - mode_col) < 0.5, coup_row[k : k + 1, :], 0.0)
        whole = tab[T_SAME : T_SAME + 128, :] * (forth + back)
        high = whole.astype(jnp.bfloat16)
        gg[k * 128 : (k + 1) * 128, :128] = high
        gg[k * 128 : (k + 1) * 128, 128:] = (whole - high.astype(jnp.float32)).astype(jnp.bfloat16)

    lane2 = lax.broadcasted_iota(jnp.int32, (1, 256), 1)
    first = lax.rem(lane2 // 32, 2) == 0
    real = lax.rem(lane2, 32) < 30

    def back_to_cells(sem, carried):
        weighted = spec[...] * dinv[...]
        own = total(spec[...] * weighted)
        cells = jnp.where(lane2 == GAMMA, own, dot(h_ref[...], weighted))
        for r in range(2):
            rsend[carried, pl.ds(r, 256, stride=2), :] = cells[:, r * 128 : (r + 1) * 128]
        mine = pair_rows(me)

        everyone(
            lambda c, m, d, n: remote(rsend.at[carried, pair_rows(n)], rrecv.at[carried, mine], sem, (c, m))
        )
        local(rsend.at[carried, pair_rows(cell)], rrecv.at[carried, mine], sem)

    landed(frecv.at[0], 0)
    arrived = [
        jnp.concatenate([frecv[0, pl.ds(hh * 256 + r, 128, stride=2), :] for r in range(2)], 1) for hh in range(2)
    ]
    even = jnp.where(first, arrived[0], pltpu.roll(arrived[1], 32, 1))
    odd = jnp.where(first, pltpu.roll(arrived[0], 224, 1), arrived[1])
    spec[...] = dot(both_ref[...], jnp.concatenate([even, odd], 0))
    back_to_cells(1, 0)

    def turned_ends(src, dst):
        dst[64:576, :] = src
        dst[0:64, :] = pltpu.roll(src[448:512], 64, 1)
        dst[576:640, :] = pltpu.roll(src[0:64], 64, 1)

    w0, w1, w2, iw0 = [tab[T_W + d : T_W + d + 1, :] for d in range(4)]
    row64 = lax.broadcasted_iota(jnp.int32, (64, 128), 0)
    lane64 = lax.broadcasted_iota(jnp.int32, (64, 128), 1)
    landed(a_all.at[pl.ds(0, 4)], 9)
    slot = 1 + 2 * mode + core
    for which, at in enumerate((slot, slot + 1 - 2 * core, slot - 1 + 2 * core)):
        aj[which] = dot_dims(a_all[at], spread_ref[...], 0, 0)
    for k in range(4):
        turned_ends(aj[0, :, k * 128 : (k + 1) * 128], ext)

        def faces(g, carry):
            at = pl.multiple_of(g * 64, 64)
            here = pl.ds(at, 64)
            a = ext[pl.ds(at + 64, 64), :]
            up, down = ext[pl.ds(at + 128, 64), :], ext[pl.ds(at, 64), :]
            sib, oth = aj[1, here, k * 128 : (k + 1) * 128], aj[2, here, k * 128 : (k + 1) * 128]
            tp = jnp.where(row64 == 63, a, pltpu.roll(a, 63, 0))
            tm = jnp.where(row64 == 0, a, pltpu.roll(a, 1, 0))
            last = jnp.logical_and(g == 7, lane64 >= 64)
            start = jnp.logical_and(g == 0, lane64 < 64)
            coef[k * 6, here, :] = (0.5 * w0) * (a + sib)
            coef[k * 6 + 1, here, :] = (0.5 * w0) * (a + oth)
            coef[k * 6 + 2, here, :] = jnp.where(last, 0.0, (0.5 * w1) * (a + up))
            coef[k * 6 + 3, here, :] = jnp.where(start, 0.0, (0.5 * w1) * (a + down))
            coef[k * 6 + 4, here, :] = (0.5 * w2) * (a + tp)
            coef[k * 6 + 5, here, :] = (0.5 * w2) * (a + tm)
            return carry

        lax.fori_loop(0, 8, faces, 0)
    landed(b_in, 8)
    bt[...] = jnp.transpose(b_in[...])

    def smoothed(n):
        landed(rrecv.at[n], 1 + 2 * n)
        carried = jnp.sum(jnp.sum(rrecv[n], axis=0, keepdims=True) * jnp.where(gamma_lane, 1.0, 0.0), axis=1, keepdims=True)
        cosines_back(rrecv.at[n], tmp)
        out = sines(tmp)
        for s in range(2):
            part = pl.ds(s * 256, 256)
            field[n, part, :] = jnp.where(valid, out[:, s * 128 : (s + 1) * 128], 0.0)
            remote(field.at[n, part], zsib.at[n, part], (5 if s == 0 else 14) + n, sibling)
        return carried

    def operator(n):
        turned_ends(field[n], ext)

        def inner(g, carry):
            at = pl.multiple_of(g * 64, 64)
            here = pl.ds(at, 64)
            v = ext[pl.ds(at + 64, 64), :]
            lp, lm = v - ext[pl.ds(at + 128, 64), :], v - ext[pl.ds(at, 64), :]
            tp = v - jnp.where(row64 == 63, 0.0, pltpu.roll(v, 63, 0))
            tm = v - jnp.where(row64 == 0, 0.0, pltpu.roll(v, 1, 0))
            for k in range(4):
                acc = (
                    coef[k * 6 + 2, here, :] * lp
                    + coef[k * 6 + 3, here, :] * lm
                    + coef[k * 6 + 4, here, :] * tp
                    + coef[k * 6 + 5, here, :] * tm
                )
                if k:
                    t123[here, (k - 1) * 128 : k * 128] = acc
                else:
                    t0[here, :] = acc
            last = jnp.logical_and(g == 7, lane64 >= 64)
            start = jnp.logical_and(g == 0, lane64 < 64)
            lap = w1 * (jnp.where(last, 0.0, lp) + jnp.where(start, 0.0, lm)) + w2 * (tp + tm) - bt[here, :]
            rest[here, :] = -(v + iw0 * lap)
            return carry

        lax.fori_loop(0, 8, inner, 0, unroll=True)

        def outer(g, carry):
            here = pl.ds(pl.multiple_of(g * 64, 64), 64)
            sib = zsib[n, here, :]
            one, two = field[n, here, :] - sib, sib + rest[here, :]
            t0[here, :] += coef[0, here, :] * one + coef[1, here, :] * two
            for k in range(1, 4):
                at = slice((k - 1) * 128, k * 128)
                acc = t123[here, at] + coef[k * 6, here, :] * one + coef[k * 6 + 1, here, :] * two
                high = acc.astype(jnp.bfloat16)
                t_high[here, at] = high
                t_low[here, at] = (acc - high.astype(jnp.float32)).astype(jnp.bfloat16)
            return carry

        for s in range(2):
            landed(zsib.at[n, pl.ds(s * 256, 256)], (5 if s == 0 else 14) + n)
            lax.fori_loop(4 * s, 4 * s + 4, outer, 0, unroll=True)
        large = dot16(t_high[...], gg[...])
        img[n] = t0[...] + (large[:, :128] + (large[:, 128:] + dot16(t_low[...], gg[:, :128])))

    def to_home(f):
        for hh in range(2):
            itself = jnp.logical_and(core == mode, mode == hh)
            for lh in range(2):
                src = out_send.at[f, pl.ds(lh * 64 + hh * 32, 32)]
                dst = out_recv.at[f, pl.ds(pl.multiple_of(lh * 64 + core * 32, 32), 32)]

                @pl.when(itself)
                def _():
                    local(src, dst, 10 + f)

                @pl.when(jnp.logical_not(itself))
                def _():
                    remote(src, dst, 10 + f, (chip * 2 + mode, hh))

    rz0 = smoothed(0)
    operator(0)
    dad = total(field[0] * img[0])

    transform_t(img.at[0], tmp)
    cosines_forward(tmp, fsend.at[1], fill=dad)
    cell_rows = pair_rows(cell)
    everyone(lambda c, m, d, n: remote(fsend.at[1, pair_rows(d)], frecv.at[1, cell_rows], 2, (c, m)))
    local(fsend.at[1, pair_rows(me)], frecv.at[1, cell_rows], 2)
    out_send[0] = jnp.transpose(field[0])
    to_home(0)
    out_send[1] = jnp.transpose(img[0])
    to_home(1)

    landed(frecv.at[1], 2)
    even = frecv[1, pl.ds(0, 256, stride=2), :]
    sums = jnp.sum(even, axis=0, keepdims=True)
    dad = jnp.sum(jnp.where(gamma_lane, sums, 0.0), axis=1, keepdims=True)
    alpha0 = rz0 / dad
    image_spec = dot(h_ref[...], jnp.concatenate([even, frecv[1, pl.ds(1, 256, stride=2), :]], 1))
    spec[...] = jnp.where(real, spec[...] - alpha0 * image_spec, 0.0)
    back_to_cells(3, 1)
    bt[...] = bt[...] - alpha0 * img[0]

    rz1 = smoothed(1)
    beta = rz1 / rz0
    out_send[2] = jnp.transpose(field[1])
    to_home(2)
    operator(1)
    dad = total((field[1] + beta * field[0]) * (img[1] + beta * img[0]))
    sum_out[...] = jnp.broadcast_to(dad, (8, 128))
    sum_in[pl.ds(me, 1), :] = jnp.broadcast_to(dad, (1, 128))
    everyone(lambda c, m, d, n: remote(sum_out.at[pl.ds(0, 1)], sum_in.at[pl.ds(me, 1)], 4, (c, m)))
    out_send[3] = jnp.transpose(img[1])
    to_home(3)
    landed(sum_in.at[pl.ds(0, 255)], 4)
    alpha1 = rz1 / jnp.sum(sum_in[...], axis=0, keepdims=True)[:, :1]
    both_steps = alpha0 + alpha1 * beta
    for f in range(4):
        landed(out_recv.at[f], 10 + f)
    y_ref[0] = both_steps * out_recv[0] + alpha1 * out_recv[2]
    y_ref[1] = xp[...] - both_steps * out_recv[1] - alpha1 * out_recv[3]

    for n in range(2):
        sent(fsend.at[n, pl.ds(0, 510)], 2 * n)
        sent(rsend.at[n, pl.ds(0, 510)], 1 + 2 * n)
        sent(field.at[n, pl.ds(0, 256)], 5 + n)
        sent(field.at[n, pl.ds(256, 256)], 14 + n)
    sent(sum_in.at[pl.ds(0, 255)], 4)
    sent(a_all.at[pl.ds(0, 4)], 9)

    @pl.when(core == mode)
    def _():
        sent(xp.at[pl.ds(0, 64)], 8)
        for f in range(4):
            sent(out_send.at[f, pl.ds(0, 64)], 10 + f)

    @pl.when(core != mode)
    def _():
        sent(xp, 8)
        for f in range(4):
            sent(out_send.at[f], 10 + f)


def unpack(y_ref, *out_refs):
    for n, out_ref in enumerate(out_refs):
        for e in range(2):
            for lh in range(2):
                at = lh * 64 + e * 32
                out_ref[:, e, lh * 512 : (lh + 1) * 512] = y_ref[n, at : at + 30, :]


def on_device(right_side, stiffness, pairing, coupling):
    consts = [jnp.asarray(v) for v in tables()]
    shape = jax.ShapeDtypeStruct((30, 2, 1024), jnp.float32)
    vmem = pl.BlockSpec(memory_space=pltpu.VMEM)
    f32 = jnp.float32
    far = pl.BlockSpec(memory_space=pltpu.HBM)
    operands = (right_side.reshape(30, 2, 1024), stiffness, pairing, coupling, *consts)
    scratch = [pltpu.VMEM(v.shape, v.dtype) for v in operands] + [
        pltpu.VMEM((128, 512), f32),
        pltpu.VMEM((128, 512), f32),
        pltpu.VMEM((2, 8, 512), f32),
        pltpu.VMEM((6, 8, 512), f32),
        pltpu.VMEM((2,) + FIELD, f32),
        pltpu.VMEM((2,) + FIELD, f32),
        pltpu.VMEM((2,) + FIELD, f32),
        pltpu.VMEM((2,) + FIELD, f32),
        pltpu.VMEM((8, 128), f32),
        pltpu.VMEM((256, 128), f32),
        pltpu.VMEM((2,) + FIELD, f32),
        pltpu.VMEM((2,) + FIELD, f32),
        pltpu.VMEM((640, 128), f32),
        pltpu.VMEM((24,) + FIELD, f32),
        pltpu.VMEM(FIELD, f32),
        pltpu.VMEM((512, 384), f32),
        pltpu.VMEM(FIELD, f32),
        pltpu.VMEM(FIELD, f32),
        pltpu.VMEM((2,) + FIELD, f32),
        pltpu.VMEM((512, 384), jnp.bfloat16),
        pltpu.VMEM((512, 384), jnp.bfloat16),
        pltpu.VMEM((384, 256), jnp.bfloat16),
        pltpu.VMEM((256, 256), f32),
        pltpu.VMEM((256, 256), f32),
        pltpu.VMEM(FIELD, f32),
        pltpu.VMEM((4, 128, 512), f32),
        pltpu.VMEM((4, 128, 512), f32),
        pltpu.VMEM((3, 512, 512), f32),
        pltpu.SemaphoreType.DMA((16,)),
        pltpu.SemaphoreType.DMA((16,)),
        pltpu.SemaphoreType.DMA((11,)),
    ]
    packed = pl.pallas_call(
        kernel,
        out_shape=jax.ShapeDtypeStruct((2, 128, 512), f32),
        in_specs=[far] * 11,
        out_specs=vmem,
        scratch_shapes=scratch,
        compiler_params=pltpu.CompilerParams(
            collective_id=0, has_side_effects=True, vmem_limit_bytes=60 * 1024 * 1024
        ),
    )(*operands)
    x, r = pl.pallas_call(unpack, out_shape=(shape, shape), in_specs=[vmem], out_specs=(vmem, vmem))(packed)
    return x.reshape(right_side.shape), r.reshape(right_side.shape)


def solution(mesh):
    placed = P("mode", None, "circ", None)
    return jax.shard_map(
        on_device,
        mesh=mesh,
        in_specs=(placed, P(None, "circ", None), P(), P()),
        out_specs=(placed, placed),
        check_vma=False,
    )
```
